32 devices in a mesh: lvl: 4 (over z), col: 8 (over y, x, core).
Axes of the slice: x: 2, y: 2, z: 4, core: 2. Of those that a mesh axis runs over, the one named last changes fastest.
Arguments:
- rhs: float32 [4, 1536, 128], P('lvl', 'col'), may hold values from -6 to 6
- panel: bfloat16 [4, 2, 1536, 1536], P('lvl', None, 'col'), may hold values from -0.078125 to 0.078125
- inverse_t: bfloat16 [4, 1536, 1536], P('lvl', 'col'), as said below
- pattern: int32 [4, 2, 12, 12], P('lvl'), may hold values 0 or 1
Outputs:
- sample: float32 [4, 1536, 128], P('lvl', 'col')
- solution: float32 [4, 1536, 128], P('lvl', 'col')
The draws below stay inside these ranges and needn't reach their ends.
Inputs may be any that keep to these rules, and one draw needn't show every extreme that they name: `pattern`: 1 marks a 128 x 128 tile of a panel slot that is structurally nonzero. Each inverse_t[s] is upper triangular with a positive diagonal.
All inputs are finite; a program needn't handle non-finite values.
Results may differ from the reference program's by a relative error of at most 0.035.
Values may be sent and summed in bfloat16 or wider, within the bound.
No kernel may reach another device: no remote copies, remote signals or barrier semaphores. Data moves between devices by JAX's collectives and lax.ppermute only.
A program may use at most 64 MiB of HBM per device.

```python
import jax
import jax.numpy as jnp
from jax import lax

NB = 1536
BLOCK = 128
NRHS = 128
NSUP = 4
ANC = 2
KB = 12
ROWS = 192
N_COL = 8


def draw_inverse_t(key, part):
    off_key, diag_key = jax.random.split(jax.random.fold_in(key, 11))
    full_shape = (NSUP, NB, NB)
    row_ids = lax.broadcasted_iota(jnp.int32, full_shape, 1)
    col_ids = lax.broadcasted_iota(jnp.int32, full_shape, 2)
    spread = jax.random.normal(off_key, full_shape, jnp.float32) * 0.6 * (1.0 / NB) ** 0.5
    diagonal = jax.random.uniform(diag_key, (NSUP, NB, 1), jnp.float32, 0.8, 1.4)
    triangle = jnp.where(col_ids > row_ids, spread, 0.0) + jnp.where(col_ids == row_ids, diagonal, 0.0)
    return triangle.astype(jnp.bfloat16)


def place_ends(result, own_key, smallest, largest):
    longest = result.shape.index(max(result.shape))
    spots = []
    for shift in (0, 1):
        where = [jax.random.randint(jax.random.fold_in(own_key, axis), (), 0, length) for axis, length in enumerate(result.shape)]
        where[longest] = (where[longest] + shift) % result.shape[longest]
        spots.append(tuple(where))
    return result.at[spots[0]].set(smallest).at[spots[1]].set(largest)


def block_scale(own_key, dims, shards, least, high):
    factor_of, own = 1.0, jax.random.fold_in(own_key, 6)
    for dim, shards_of in shards:
        steps = jnp.exp(jax.random.uniform(jax.random.fold_in(own, dim), (shards_of,), jnp.float32, least / len(shards), high / len(shards)))
        factor_of = factor_of * jnp.repeat(steps, dims[dim] // shards_of).reshape([-1 if axis == dim else 1 for axis in range(len(dims))])
    return factor_of


def bell_draw(key, dims, width, reach, pieces=(), dtype=jnp.bfloat16):
    array = width * jax.random.normal(key, dims, jnp.float32)
    if pieces:
        array = array * block_scale(key, dims, pieces, -0.22, 0.18)
    return jnp.clip(array, -reach, reach).astype(dtype)


def setup_inputs(seed: int = 0) -> dict:
    key_list = jax.random.split(jax.random.key(seed), 5)
    rhs = bell_draw(key_list[0], (NSUP, NB, NRHS), 1.0, 6.0, ((0, 4), (1, 8)), jnp.float32)
    panel = bell_draw(key_list[1], (NSUP, ANC, NB, NB), (4 * NB) ** -0.5, 0.078125, ((0, 4), (2, 8)))
    inverse_t = draw_inverse_t(jax.random.fold_in(key_list[4], 71), 0)
    pattern = place_ends((jax.random.randint(key_list[3], (NSUP, ANC, KB, KB), 0, 4) < 3).astype(jnp.int32), jax.random.fold_in(key_list[3], 1), 0, 1)
    return {"rhs": rhs, "panel": panel, "inverse_t": inverse_t, "pattern": pattern}


def trailing_ones(position):
    ones_count = 0
    while position % 2 == 1:
        ones_count += 1
        position = position // 2
    return ones_count


def ancestor_list(node_id, node_total):
    chain_list = []
    while node_id != node_total - 1:
        depth_now = trailing_ones(node_id)
        step_size = 2 ** depth_now
        if (node_id // (2 * step_size)) % 2 == 0:
            node_id = node_id + step_size
        else:
            node_id = node_id - step_size
        chain_list.append(node_id)
    return chain_list


def rounded(quantity):
    return lax.optimization_barrier(quantity.astype(jnp.bfloat16)).astype(jnp.float32)


def reference(rhs, panel, inverse_t, pattern):
    levels = NSUP.bit_length() - 1
    chains = [ancestor_list(node_id, NSUP) for node_id in range(NSUP)]

    def slot_block(node_id, slot_pos):
        grown_mask = jnp.repeat(jnp.repeat(pattern[node_id, slot_pos], BLOCK, axis=0), BLOCK, axis=1)
        return panel[node_id, slot_pos] * grown_mask.astype(jnp.bfloat16)

    incoming = [jnp.zeros((NB, NRHS), jnp.float32) for node_id in range(NSUP)]
    sample = [None] * NSUP
    for section_num in range(levels + 1):
        for node_id in range(NSUP):
            if trailing_ones(node_id) != section_num:
                continue
            residual = (rhs[node_id] - incoming[node_id]).astype(jnp.bfloat16)
            inv_parts = inverse_t[node_id].reshape(N_COL, ROWS, NB).astype(jnp.float32)
            res_parts = residual.reshape(N_COL, ROWS, NRHS).astype(jnp.float32)
            part_sums = jnp.einsum('cri,crn->cin', inv_parts, res_parts)
            solved = jnp.sum(rounded(part_sums), axis=0)
            sample[node_id] = solved
            solved_half = solved.astype(jnp.bfloat16)
            for slot_pos, upper_id in enumerate(chains[node_id]):
                incoming[upper_id] = incoming[upper_id] + jnp.dot(slot_block(node_id, slot_pos), solved_half, preferred_element_type=jnp.float32)

    solution = [None] * NSUP
    solution_half = [None] * NSUP
    for section_num in range(levels, -1, -1):
        for node_id in range(NSUP):
            if trailing_ones(node_id) != section_num:
                continue
            chain_list = chains[node_id]
            if len(chain_list) > 0:
                depth_now = len(chain_list)
                blocks = jnp.stack([slot_block(node_id, slot_pos) for slot_pos in range(depth_now)]).astype(jnp.float32)
                ancestry = jnp.stack([solution_half[upper_id] for upper_id in chain_list]).astype(jnp.float32)
                part_sums = jnp.einsum('kcrn,kcrm->cnm', blocks.reshape(depth_now, N_COL, ROWS, NB), ancestry.reshape(depth_now, N_COL, ROWS, NRHS))
                adjoint = jnp.sum(rounded(part_sums), axis=0)
                back_full = sample[node_id] - adjoint
            else:
                back_full = sample[node_id]
            solved = jnp.dot(inverse_t[node_id], back_full.astype(jnp.bfloat16), preferred_element_type=jnp.float32)
            solution[node_id] = solved
            solution_half[node_id] = solved.astype(jnp.bfloat16)
    return jnp.stack(sample), jnp.stack(solution)
```

```python
import jax
import jax.numpy as jnp
from jax import lax
from jax.sharding import PartitionSpec as P

F32 = jnp.float32
BF16 = jnp.bfloat16


def trailing_ones(node):
    ones = 0
    while node % 2 == 1:
        ones += 1
        node //= 2
    return ones


def level_rank(device_pos, levels):
    running = jnp.zeros((), jnp.int32)
    for exponent in range(1, levels + 1):
        running = running + ((device_pos + 1) % 2**exponent == 0).astype(jnp.int32)
    return running


def child_pairs(section, members):
    reach = 2 ** (section - 1)
    parents = [node for node in range(members - 1) if trailing_ones(node) == section]
    left = [(node - reach, node) for node in parents]
    right = [(node + reach, node) for node in parents]
    return left, right


def expand_pattern(pattern_own, row_start, row_count, full_width):
    tile_count = pattern_own.shape[1]
    tile_size = full_width // tile_count
    row_ids = row_start + lax.iota(jnp.int32, row_count)
    row_pick = (row_ids[:, None] // tile_size == lax.iota(jnp.int32, tile_count)[None, :]).astype(BF16)
    col_pick = (
        lax.iota(jnp.int32, full_width)[None, :] // tile_size == lax.iota(jnp.int32, tile_count)[:, None]
    ).astype(BF16)
    row_mask = jnp.einsum("rb,kbc->krc", row_pick, pattern_own.astype(BF16), preferred_element_type=F32)
    return jnp.einsum("krc,cn->krn", row_mask.astype(BF16), col_pick, preferred_element_type=F32).astype(BF16)


def on_device(rhs, panel, inverse_t, pattern):
    members = lax.axis_size("lvl")
    cols = lax.axis_size("col")
    levels = members.bit_length() - 1
    root, heir = members - 1, members // 2 - 1
    lvl_pos = lax.axis_index("lvl")
    col_pos = lax.axis_index("col")
    core = col_pos % 2
    row_count, rhs_count = rhs.shape[1:]
    half = rhs_count // 2
    full_width = inverse_t.shape[2]
    height = level_rank(lvl_pos, levels)

    def swap(x, offset):
        return lax.ppermute(x, "col", [(i, i ^ offset) for i in range(cols)])

    def along(x, pairs):
        return lax.ppermute(x, "lvl", pairs)

    def col_sum(partial):
        terms = partial.astype(BF16)
        low, high = terms[:half], terms[half:]
        keep = jnp.where(core == 0, low, high)
        give = jnp.where(core == 0, high, low)
        chip = (keep.astype(F32) + swap(give, 1).astype(F32)).astype(BF16)
        total = chip.astype(F32)
        for offset in range(2, cols, 2):
            total = total + swap(chip, offset).astype(F32)
        own = total.astype(BF16)
        other = swap(own, 1)
        return jnp.concatenate([jnp.where(core == 0, own, other), jnp.where(core == 0, other, own)], axis=0)

    def own_rows(whole):
        return lax.dynamic_slice_in_dim(whole, col_pos * row_count, row_count, 1).T.astype(F32)

    inverse_own = inverse_t[0]
    right_side = rhs[0]
    root_inverse = along(inverse_own, [(root, heir)])
    root_rhs = along(right_side, [(root, heir)])
    factor = panel[0] * expand_pattern(pattern[0], col_pos * row_count, row_count, full_width)

    def down_solve(inverse, residual):
        return col_sum(jnp.einsum("ri,rn->ni", inverse, residual.astype(BF16), preferred_element_type=F32))

    def up_solve(inverse, back):
        return jnp.einsum("ri,ni->rn", inverse, back, preferred_element_type=F32)

    samples = [None] * levels
    gathered = None
    for section in range(levels):
        if section > 0:
            left, right = child_pairs(section, members)
            sent = pushed.astype(BF16)
            gathered = along(sent, left).astype(F32) + along(sent, right).astype(F32)
        residual = right_side if gathered is None else right_side - gathered[0]
        samples[section] = down_solve(inverse_own, residual)
        pushed = jnp.einsum("krn,mn->krm", factor[: levels - section], samples[section], preferred_element_type=F32)
        if gathered is not None:
            pushed = pushed + gathered[1:]
    root_sample = down_solve(root_inverse, root_rhs - pushed[0])
    root_answer = up_solve(root_inverse, root_sample)
    sample = own_rows(samples[0])
    for section in range(1, levels):
        sample = jnp.where(height == section, own_rows(samples[section]), sample)

    ancestry = root_answer.astype(BF16)[None]
    answer = None
    for section in range(levels - 1, -1, -1):
        if section < levels - 1:
            left, right = child_pairs(section + 1, members)
            sent = jnp.concatenate([solved.astype(BF16)[None], ancestry], axis=0)
            ancestry = along(sent, [(b, a) for a, b in left]) + along(sent, [(b, a) for a, b in right])
        adjoint = col_sum(jnp.einsum("krn,krm->mn", factor[: levels - section], ancestry, preferred_element_type=F32))
        back = (samples[section].astype(F32) - adjoint.astype(F32)).astype(BF16)
        solved = up_solve(inverse_own, back)
        answer = solved if answer is None else jnp.where(height == section, solved, answer)
    root_out = along(jnp.stack([own_rows(root_sample), root_answer]), [(heir, root)])
    at_root = lvl_pos == root
    sample = jnp.where(at_root, root_out[0], sample)
    answer = jnp.where(at_root, root_out[1], answer)
    return (sample[None], answer[None])


def solution(mesh):
    in_specs = (
        P("lvl", "col", None),
        P("lvl", None, "col", None),
        P("lvl", "col", None),
        P("lvl", None, None, None),
    )
    out_specs = (P("lvl", "col", None), P("lvl", "col", None))
    return jax.shard_map(
        on_device, mesh=mesh, in_specs=in_specs, out_specs=out_specs, check_vma=False
    )
```

```python
import jax
import jax.numpy as jnp
from jax import lax
from jax.sharding import PartitionSpec as P

F32 = jnp.float32
BF16 = jnp.bfloat16


def trailing_ones(node):
    ones = 0
    while node % 2 == 1:
        ones += 1
        node //= 2
    return ones


def child_links(section, members):
    reach = 2 ** (section - 1)
    parents = [node for node in range(members - 1) if trailing_ones(node) == section]
    return [(node - reach, node) for node in parents], [(node + reach, node) for node in parents]


def expand_pattern(pattern_own, row_start, row_count, full_width):
    tile_count = pattern_own.shape[1]
    tile_size = full_width // tile_count
    row_ids = row_start + lax.iota(jnp.int32, row_count)
    row_pick = (row_ids[:, None] // tile_size == lax.iota(jnp.int32, tile_count)[None, :]).astype(BF16)
    col_pick = (
        lax.iota(jnp.int32, full_width)[None, :] // tile_size == lax.iota(jnp.int32, tile_count)[:, None]
    ).astype(BF16)
    row_mask = jnp.einsum("rb,kbc->krc", row_pick, pattern_own.astype(BF16), preferred_element_type=F32)
    return jnp.einsum("krc,cn->krn", row_mask.astype(BF16), col_pick, preferred_element_type=F32).astype(BF16)


def xor_order(blocks, mask, axis=0):
    count = blocks.shape[axis]
    step = 1
    while step < count:
        flipped = jnp.stack(
            [lax.index_in_dim(blocks, b ^ step, axis, keepdims=False) for b in range(count)], axis=axis
        )
        blocks = jnp.where((mask // step) % 2 == 1, flipped, blocks)
        step *= 2
    return blocks


def on_device(rhs, panel, inverse_t, pattern):
    members = lax.axis_size("lvl")
    cols = lax.axis_size("col")
    levels = members.bit_length() - 1
    root, heir = members - 1, members // 2 - 1
    chips = cols // 2
    lanes = 1 << ((chips.bit_length() - 1) // 2)
    lvl_pos = lax.axis_index("lvl")
    col_pos = lax.axis_index("col")
    core, lane, row = col_pos % 2, col_pos // 2 % lanes, col_pos // (2 * lanes)
    row_count, rhs_count = rhs.shape[1:]
    full_width = inverse_t.shape[2]
    group = rhs_count // (2 * lanes)
    blocks = 2 * lanes
    own_group = core * lanes + lane
    levels_of = [trailing_ones(node) for node in range(members)]
    leaves = [node for node in range(members) if levels_of[node] == 0]
    inner = [node for node in range(members - 1) if levels_of[node] > 0]

    def across(x, offset, planes):
        pairs = [(p * cols + c, p * cols + (c ^ offset)) for p in planes for c in range(cols)]
        return lax.ppermute(x, ("lvl", "col"), pairs)

    def along(x, links, offset=0):
        pairs = [(a * cols + c, b * cols + (c ^ offset)) for a, b in links for c in range(cols)]
        return lax.ppermute(x, ("lvl", "col"), pairs)

    def down(links):
        return [(b, a) for a, b in links]

    def chip_sum(mine):
        total = mine.astype(F32)
        for chip in range(1, chips):
            got = across(mine, 2 * chip, leaves)
            turned = jnp.stack([got[i ^ (chip % lanes)] for i in range(lanes)])
            total = total + turned.astype(F32)
        return total

    def row_sum(partial, planes):
        terms = partial.astype(BF16)
        total = terms.astype(F32)
        for offset in range(2 * lanes, cols, 2 * lanes):
            total = total + across(terms, offset, planes).astype(F32)
        return total

    def spread_rows(matrix, planes):
        lane_parts = [matrix] + [across(matrix, 2 * i, planes) for i in range(1, lanes)]
        return jnp.stack([part for own in lane_parts for part in (own, across(own, 1, planes))])

    def turn_blocks(parts, planes):
        got = [parts[..., 0, :, :]] + [across(parts[..., b, :, :], b, planes) for b in range(1, blocks)]
        return jnp.stack(got, axis=-3)

    def to_blocks(vector):
        by_group = xor_order(vector.T.reshape(blocks, group, row_count), own_group)
        return by_group.reshape(2, lanes, group, row_count).swapaxes(0, 1).reshape(blocks, group, row_count)

    def from_blocks(parts):
        by_group = parts.reshape(lanes, 2, group, row_count).swapaxes(0, 1).reshape(blocks, group, row_count)
        return xor_order(by_group, own_group).reshape(rhs_count, row_count).T

    inverse_own = inverse_t[0]
    factor = panel[0] * expand_pattern(pattern[0], col_pos * row_count, row_count, full_width)

    first = xor_order(rhs[0].T.reshape(blocks, group, row_count), own_group).astype(BF16)
    partial = jnp.einsum("bnr,ri->bni", first, inverse_own, preferred_element_type=F32).astype(BF16)
    got = across(partial[lanes:], 1, leaves)
    chip_part = (partial[:lanes].astype(F32) + got.astype(F32)).astype(BF16)
    leaf_half = chip_sum(chip_part).astype(BF16)
    factor_pair = jnp.stack([factor, across(factor, 1, leaves)], axis=1)
    pushed = jnp.einsum("lni,kjri->kjlnr", leaf_half, factor_pair, preferred_element_type=F32).astype(BF16)

    root_inverse = along(inverse_own, [(root, heir)])
    root_rhs = along(rhs[0], [(root, heir)])
    inner_inverse = spread_rows(inverse_own, inner)
    inner_factor = jnp.stack([spread_rows(factor[k], inner) for k in range(levels - 1)])
    root_spread = spread_rows(root_inverse, [heir])
    inner_rhs = turn_blocks(jnp.stack([to_blocks(rhs[0]), to_blocks(root_rhs)]), inner)

    samples = {}
    for section in range(1, levels):
        left, right = child_links(section, members)
        nodes = [node for node in inner if levels_of[node] == section]
        if section == 1:
            parts = [
                along(pushed[:, :, i], left, 2 * i).astype(F32) + along(pushed[:, :, i], right, 2 * i).astype(F32)
                for i in range(lanes)
            ]
            gathered = jnp.stack(parts, axis=1).reshape(levels, blocks, group, row_count)
        else:
            sent = pushed.astype(BF16)
            gathered = along(sent, left).astype(F32) + along(sent, right).astype(F32)
        residual = (inner_rhs[0] - gathered[0]).astype(BF16)
        samples[section] = row_sum(
            jnp.einsum("bnr,bri->ni", residual, inner_inverse, preferred_element_type=F32), nodes
        )
        pushed = gathered[1:] + jnp.einsum(
            "ni,kbri->kbnr", samples[section].astype(BF16), inner_factor[: levels - section], preferred_element_type=F32
        )
    residual = (inner_rhs[1] - pushed[0]).astype(BF16)
    root_sample = row_sum(jnp.einsum("bnr,bri->ni", residual, root_spread, preferred_element_type=F32), [heir])
    root_answer = jnp.einsum("ni,bri->bnr", root_sample.astype(BF16), root_spread, preferred_element_type=F32)

    answers = {}
    ancestry = root_answer.astype(BF16)[None]
    for section in range(levels - 1, 0, -1):
        nodes = [node for node in inner if levels_of[node] == section]
        if section < levels - 1:
            left, right = child_links(section + 1, members)
            ancestry = along(sent, down(left)) + along(sent, down(right))
        adjoint = row_sum(
            jnp.einsum("kbnr,kbri->ni", ancestry, inner_factor[: levels - section], preferred_element_type=F32), nodes
        )
        back = (samples[section] - adjoint).astype(BF16)
        answers[section] = jnp.einsum("ni,bri->bnr", back, inner_inverse, preferred_element_type=F32)
        sent = jnp.concatenate([answers[section].astype(BF16)[None], ancestry], axis=0)

    left, right = child_links(1, members)
    sent = sent.reshape(levels, lanes, 2, group, row_count)
    ancestry = jnp.stack(
        [along(sent[:, i], down(left), 2 * i) + along(sent[:, i], down(right), 2 * i) for i in range(lanes)], axis=2
    )
    partial = jnp.einsum("kjlnr,kjri->lni", ancestry, factor_pair, preferred_element_type=F32).astype(BF16)
    back = (leaf_half.astype(F32) - chip_sum(partial)).astype(BF16)

    def whole(half):
        both = jnp.concatenate([half, across(half, 1, leaves)], axis=0)
        return xor_order(both, own_group).reshape(rhs_count, full_width)

    leaf_answer = jnp.einsum("ri,ni->rn", inverse_own, whole(back), preferred_element_type=F32)
    leaf_sample = lax.dynamic_slice_in_dim(whole(leaf_half), col_pos * row_count, row_count, 1).T.astype(F32)

    def own_blocks(vector):
        here = lax.dynamic_slice_in_dim(vector, row * blocks * row_count, blocks * row_count, 1)
        return xor_order(here.reshape(group, blocks, row_count).swapaxes(0, 1), lane * 2 + core)

    height = jnp.asarray(levels_of)[lvl_pos]
    inner_sample, inner_answer = samples[1], answers[1]
    for section in range(2, levels):
        inner_sample = jnp.where(height == section, samples[section], inner_sample)
        inner_answer = jnp.where(height == section, answers[section], inner_answer)
    parts = turn_blocks(
        jnp.stack([own_blocks(inner_sample), inner_answer, own_blocks(root_sample), root_answer]), inner
    )
    results = jnp.stack([from_blocks(parts[n]) for n in range(4)])
    root_results = along(results[2:], [(heir, root)])
    at_leaf, at_root = height == 0, lvl_pos == root
    sample = jnp.where(at_leaf, leaf_sample, jnp.where(at_root, root_results[0], results[0]))
    answer = jnp.where(at_leaf, leaf_answer, jnp.where(at_root, root_results[1], results[1]))
    return (sample[None], answer[None])


def solution(mesh):
    in_specs = (
        P("lvl", "col", None),
        P("lvl", None, "col", None),
        P("lvl", "col", None),
        P("lvl", None, None, None),
    )
    out_specs = (P("lvl", "col", None), P("lvl", "col", None))
    return jax.shard_map(
        on_device, mesh=mesh, in_specs=in_specs, out_specs=out_specs, check_vma=False
    )
```

```python
import jax
import jax.numpy as jnp
from jax import lax
from jax.experimental import pallas as pl
from jax.experimental.pallas import tpu as pltpu
from jax.sharding import PartitionSpec as P

F32 = jnp.float32
BF16 = jnp.bfloat16


def trailing_ones(node):
    ones = 0
    while node % 2 == 1:
        ones += 1
        node //= 2
    return ones


def child_links(section, members):
    reach = 2 ** (section - 1)
    parents = [node for node in range(members) if trailing_ones(node) == section]
    links = [[(node - reach, node) for node in parents], [(node + reach, node) for node in parents]]
    return [[(a, b) for a, b in side if a < members] for side in links if any(a < members for a, b in side)]


def mm(a, b):
    return jnp.dot(a, b, preferred_element_type=F32)


def mmt(a, b):
    return lax.dot_general(a, b, (((1,), (1,)), ((), ())), preferred_element_type=F32)


class Columns:
    def __init__(self, array, start, count):
        self.array, self.start, self.count = array, start, count


def call(body, outs, args, scratch=()):
    single = isinstance(outs, tuple)
    shapes = [outs] if single else outs
    specs, arrays, buffers, copies = [], [], [], []
    for n, arg in enumerate(args):
        if isinstance(arg, Columns):
            rows = arg.array.shape[0]
            pieces = 2 if rows % 32 == 0 else 1
            copies.append((n, arg, rows // pieces, pieces))
            buffers += [pltpu.VMEM((rows, arg.count), arg.array.dtype), pltpu.SemaphoreType.DMA((pieces,))]
            specs.append(pl.BlockSpec(memory_space=pl.ANY))
            arrays.append(arg.array)
        else:
            specs.append(pl.BlockSpec(memory_space=pltpu.VMEM))
            arrays.append(arg)

    def kernel(*refs):
        inputs = list(refs[: len(args)])
        results = refs[len(args) : len(args) + len(shapes)]
        held = refs[len(args) + len(shapes) :]
        started = []
        for m, (n, arg, rows, pieces) in enumerate(copies):
            source, buffer, sems = inputs[n], held[2 * m], held[2 * m + 1]
            for p in range(pieces):
                span = pl.ds(p * rows, rows)
                started.append(
                    pltpu.make_async_copy(
                        source.at[span, pl.ds(arg.start, arg.count)], buffer.at[span], sems.at[p]
                    )
                )
            inputs[n] = buffer
        for copy in started:
            copy.start()

        def ready():
            for copy in started:
                copy.wait()

        body(ready, inputs, results, *held[2 * len(copies) :])

    moved = sum(a.size * a.dtype.itemsize for a in arrays)
    result = pl.pallas_call(
        kernel,
        out_shape=[jax.ShapeDtypeStruct(shape, dtype) for shape, dtype in shapes],
        in_specs=specs,
        out_specs=[pl.BlockSpec(memory_space=pltpu.VMEM) for _ in shapes],
        scratch_shapes=buffers + list(scratch),
        compiler_params=pltpu.CompilerParams(vmem_limit_bytes=24 << 20),
        cost_estimate=pl.CostEstimate(flops=1 << 28, bytes_accessed=moved, transcendentals=0),
    )(*arrays)
    return result[0] if single else result


def on_device(rhs, panel, inverse_t, pattern):
    members = lax.axis_size("lvl")
    cols = lax.axis_size("col")
    levels = members.bit_length() - 1
    last = levels - 1
    chips = cols // 2
    lanes = 1 << ((chips.bit_length() - 1) // 2)
    row_count, rhs_count = rhs.shape[1:]
    width = inverse_t.shape[2]
    blocks = 2 * lanes
    group = rhs_count // blocks
    half = rhs_count // 2
    levels_of = [trailing_ones(node) for node in range(members)]
    nodes_at = [[node for node in range(members) if levels_of[node] == s] for s in range(levels + 1)]
    leaves = nodes_at[0]
    inner = [node for node in range(members) if levels_of[node] > 0]

    def place():
        at = lax.axis_index("col")
        core, lane = at % 2, at // 2 % lanes
        return at // blocks, lane, core, core * lanes + lane

    def height():
        at, rank = lax.axis_index("lvl"), 0
        for s in range(1, levels + 1):
            rank = rank + ((at + 1) % 2**s == 0).astype(jnp.int32)
        return rank

    def across(x, offset, planes):
        pairs = [(p * cols + c, p * cols + (c ^ offset)) for p in planes for c in range(cols)]
        return lax.ppermute(x, ("lvl", "col"), pairs)

    def along(x, links, offset=0):
        pairs = [(a * cols + c, b * cols + (c ^ offset)) for a, b in links for c in range(cols)]
        return lax.ppermute(x, ("lvl", "col"), pairs)

    def down(links):
        return [(b, a) for a, b in links]

    def after(x, *earlier):
        return lax.optimization_barrier((x, *earlier))[0]

    def over_chips(mine):
        return [mine] + [across(mine, 2 * chip, leaves) for chip in range(1, chips)]

    def over_rows(mine, planes):
        return [mine] + [across(mine, offset, planes) for offset in range(2 * lanes, cols, 2 * lanes)]

    def chip_total(refs):
        parts = []
        for i in range(lanes):
            total = refs[0][i * group : (i + 1) * group, :].astype(F32)
            for chip in range(1, chips):
                k = i ^ (chip % lanes)
                total = total + refs[chip][k * group : (k + 1) * group, :].astype(F32)
            parts.append(total)
        return jnp.concatenate(parts, axis=0)

    def row_total(refs):
        total = refs[0][...].astype(F32)
        for ref in refs[1:]:
            total = total + ref[...].astype(F32)
        return total

    def total_of(parts):
        total = parts[0]
        for part in parts[1:]:
            total = total + part
        return total

    def groups(b):
        return pl.ds(pl.multiple_of((b ^ place()[3]) * group, group), group)

    inverse_own = Columns(inverse_t[0], 0, width)
    chip_rows = len(range(0, cols, 2 * lanes))

    def leaf_first(ready, ins, outs, turned, ordered):
        turned[...] = ins[0][...].T
        for b in range(blocks):
            ordered[b * group : (b + 1) * group, :] = turned[groups(b), :]
        terms = ordered[...].astype(BF16)
        ready()
        outs[0][...] = mm(terms[:half], ins[1][...]).astype(BF16)
        outs[1][...] = mm(terms[half:], ins[1][...]).astype(BF16)

    keep, give = call(
        leaf_first,
        [((half, width), BF16)] * 2,
        [rhs[0], inverse_own],
        [pltpu.VMEM((rhs_count, row_count), F32)] * 2,
    )
    got = across(give, 1, leaves)

    tiles = pattern.shape[-1]
    tile = width // tiles
    full = levels * width + 2 * rhs_count

    def build(ready, ins, outs):
        (rhs_ref, pattern_ref, inv_ref, *panels), (out,) = ins, outs
        first_row = lax.axis_index("col") * row_count
        row_ids = lax.broadcasted_iota(jnp.int32, (row_count, tiles), 0) + first_row
        row_tile = lax.broadcasted_iota(jnp.int32, (row_count, tiles), 1)
        row_pick = ((row_ids >= row_tile * tile) & (row_ids < (row_tile + 1) * tile)).astype(F32).astype(BF16)
        col_ids = lax.broadcasted_iota(jnp.int32, (tiles, width), 1)
        col_tile = lax.broadcasted_iota(jnp.int32, (tiles, width), 0)
        col_pick = ((col_ids >= col_tile * tile) & (col_ids < (col_tile + 1) * tile)).astype(F32).astype(BF16)
        high = rhs_ref[...].astype(BF16)
        out[:, levels * width : levels * width + rhs_count] = high
        out[:, levels * width + rhs_count :] = (rhs_ref[...] - high.astype(F32)).astype(BF16)
        masks = []
        for k in range(levels):
            kept = mm(row_pick, pattern_ref[0, k].astype(F32).astype(BF16)).astype(BF16)
            masks.append(mm(kept, col_pick).astype(BF16))
        ready()
        for k in range(levels):
            block = panels[k][...] * masks[k]
            if k == last:
                block = jnp.where(height() == 0, block, inv_ref[...])
            out[:, k * width : (k + 1) * width] = block

    slots = [Columns(panel[0, k], 0, width) for k in range(levels)]
    rows_own = call(
        build, ((row_count, full), BF16), [after(rhs[0], give), pattern, inverse_own, *slots]
    )
    rows_own = after(rows_own, got)
    rows_far = across(rows_own, 1, range(members))
    rows_lanes = [across(rows_own, 2 * i, inner) for i in range(1, lanes)]
    chip_part = (keep.astype(F32) + got.astype(F32)).astype(BF16)
    terms = over_chips(chip_part)

    def factors(array, k, count=1):
        return Columns(array, k * width, count * width)

    def inverses(array):
        return Columns(array, last * width, width)

    def leaf_push(ready, ins, outs):
        solved = chip_total(ins[:chips]).astype(BF16)
        outs[0][...] = solved
        ready()
        for k in range(levels):
            for j in range(2):
                product = mmt(solved, ins[chips + j][:, k * width : (k + 1) * width]).astype(BF16)
                for i in range(lanes):
                    outs[1 + i][k, j] = product[i * group : (i + 1) * group]

    message = ((levels, 2, group, row_count), BF16)
    vector = ((blocks, group, row_count), F32)
    term = ((group, width), BF16)
    leaf_pair = [factors(rows_own, 0, levels), factors(rows_far, 0, levels)]
    leaf_half, *pushed = call(leaf_push, [((half, width), BF16)] + [message] * lanes, [*terms, *leaf_pair])
    sides = child_links(1, members)
    arrived = [along(pushed[i], links, 2 * i) for i in range(lanes) for links in sides]

    inner_rows = [rows_own, rows_far]
    for near in rows_lanes:
        inner_rows += [near, across(after(near, *arrived), 1, inner)]

    samples = {}
    for section in range(1, levels + 1):
        remain = levels - section
        count = len(arrived)

        def inner_first(ready, ins, outs):
            came, rows_of = ins[:count], ins[count:]

            def total(k, b):
                if section == 1:
                    pair = came[b // 2 * 2 : b // 2 * 2 + 2]
                    return pair[0][k, b % 2].astype(F32) + pair[1][k, b % 2].astype(F32)
                return total_of([ref[k, b].astype(F32) for ref in came])

            for k in range(remain):
                for b in range(blocks):
                    outs[1][k, b] = total(k + 1, b)
            own = lax.broadcasted_iota(jnp.int32, (group, rhs_count), 0) + place()[3] * group
            pick = (lax.broadcasted_iota(jnp.int32, (group, rhs_count), 1) == own).astype(F32).astype(BF16)
            ready()
            parts = []
            for b in range(blocks):
                both = rows_of[b][:, width:]
                side = mmt(pick, both[:, :rhs_count]) + mmt(pick, both[:, rhs_count:])
                parts.append(mm((side - total(0, b)).astype(BF16), rows_of[b][:, :width]))
            outs[0][...] = total_of(parts).astype(BF16)

        outs = [term] + ([((remain, blocks, group, row_count), F32)] if remain else [])
        own_term, *rest = call(
            inner_first,
            outs,
            [*arrived, *[Columns(rows, last * width, width + 2 * rhs_count) for rows in inner_rows]],
        )
        terms = over_rows(own_term, nodes_at[section])
        if section == 1:
            leaf_far = across(after(leaf_half, own_term), 1, leaves)
        if remain:

            def inner_push(ready, ins, outs):
                solved = row_total(ins[:chip_rows])
                more, rows_of = ins[chip_rows], ins[chip_rows + 1 :]
                outs[0][...] = solved
                short = solved.astype(BF16)
                ready()
                for k in range(remain):
                    for b in range(blocks):
                        product = mmt(short, rows_of[b][:, k * width : (k + 1) * width])
                        outs[1][k, b] = (more[k, b] + product).astype(BF16)

            samples[section], sent = call(
                inner_push,
                [((group, width), F32), ((remain, blocks, group, row_count), BF16)],
                [*terms, *rest, *[factors(rows, 0, remain) for rows in inner_rows]],
            )
            arrived = [along(sent, links) for links in child_links(section + 1, members)]

    def root_back(ready, ins, outs):
        solved = row_total(ins[:chip_rows])
        outs[0][...] = solved
        short = solved.astype(BF16)
        ready()
        for b in range(blocks):
            answer = mmt(short, ins[chip_rows + b][...])
            outs[1][b] = answer
            outs[2][0, b] = answer.astype(BF16)

    samples[levels], answer, sent = call(
        root_back,
        [((group, width), F32), vector, ((1, blocks, group, row_count), BF16)],
        [*terms, *[inverses(rows) for rows in inner_rows]],
    )

    def split_rows(ready, ins, outs):
        rank = height()
        solved = ins[0][...]
        for s in range(2, levels + 1):
            solved = jnp.where(rank == s, ins[s - 1][...], solved)
        high = solved.astype(BF16)
        stacked = jnp.concatenate([high, (solved - high.astype(F32)).astype(BF16)], axis=0)
        row, lane, core, _ = place()
        for b in range(blocks):
            start = (row * blocks + (b ^ (lane * 2 + core))) * row_count
            at = lax.broadcasted_iota(jnp.int32, (row_count, width), 0) + start
            pick = (lax.broadcasted_iota(jnp.int32, (row_count, width), 1) == at).astype(F32).astype(BF16)
            both = mmt(stacked, pick)
            outs[0][b] = both[:group] + both[group:]

    for section in range(levels - 1, 0, -1):
        remain = levels - section
        ancestry = total_of([along(sent, down(links)) for links in child_links(section + 1, members)])

        def adjoint_first(ready, ins, outs):
            ready()
            parts = []
            for b in range(blocks):
                for k in range(remain):
                    parts.append(mm(ins[0][k, b], ins[1 + b][:, k * width : (k + 1) * width]))
            outs[0][...] = total_of(parts).astype(BF16)

        own_term = call(adjoint_first, term, [ancestry, *[factors(rows, 0, remain) for rows in inner_rows]])
        terms = over_rows(own_term, nodes_at[section])
        if section == 1:
            order = [after(samples[s], own_term) for s in range(1, levels + 1)]
            sample_rows = call(split_rows, vector, order)

        def inner_back(ready, ins, outs):
            came, ins = ins[:chip_rows], ins[chip_rows:]
            (solved, anc, higher), rows_of = ins[:3], ins[3 : 3 + blocks]
            back = (solved[...] - row_total(came)).astype(BF16)
            rank = height()
            ready()
            for b in range(blocks):
                mine = mmt(back, rows_of[b][...])
                if section > 1:
                    outs[0][b] = jnp.where(rank == section, mine, higher[b])
                    outs[1][0, b] = mine.astype(BF16)
                    for k in range(remain):
                        outs[1][k + 1, b] = anc[k, b]
                else:
                    outs[b // 2][0, b % 2] = mine.astype(BF16)
                    for k in range(remain):
                        outs[b // 2][k + 1, b % 2] = anc[k, b]
                    outs[lanes + b][0] = ins[-1][b]
                    outs[lanes + b][1] = jnp.where(rank == 1, mine, higher[b])

        args = [*terms, samples[section], ancestry, answer, *[inverses(rows) for rows in inner_rows]]
        if section > 1:
            answer, sent = call(
                inner_back, [vector, ((remain + 1, blocks, group, row_count), BF16)], args
            )
        else:
            outs = [message] * lanes + [((2, group, row_count), F32)] * blocks
            results = call(inner_back, outs, [*args, sample_rows])
            sent, results = results[:lanes], results[lanes:]

    arrived = [along(sent[i], down(links), 2 * i) for i in range(lanes) for links in sides]

    def leaf_adjoint(ready, ins, outs):
        came, pair = ins[:-2], ins[-2:]
        ready()
        parts = []
        for k in range(levels):
            for j in range(2):
                anc = [came[2 * i][k, j] + came[2 * i + 1][k, j] for i in range(lanes)]
                parts.append(mm(jnp.concatenate(anc, axis=0), pair[j][:, k * width : (k + 1) * width]))
        outs[0][...] = total_of(parts).astype(BF16)

    own_term = call(leaf_adjoint, ((half, width), BF16), [*arrived, *leaf_pair])
    terms = over_chips(own_term)

    def in_order(near, far, whole):
        for b in range(blocks):
            source = near if b < lanes else far
            whole[groups(b), :] = source[b % lanes * group : (b % lanes + 1) * group, :]

    def leaf_rows(ready, ins, outs, whole):
        in_order(ins[0], ins[1], whole)
        at = lax.broadcasted_iota(jnp.int32, (row_count, width), 0) + lax.axis_index("col") * row_count
        pick = (lax.broadcasted_iota(jnp.int32, (row_count, width), 1) == at).astype(F32).astype(BF16)
        outs[0][...] = mmt(pick, whole[...])

    whole_half = [pltpu.VMEM((rhs_count, width), BF16)]
    leaf_sample = call(leaf_rows, ((row_count, rhs_count), F32), [leaf_half, leaf_far], whole_half)

    parts = [results[0]] + [across(results[b], b, inner) for b in range(1, blocks)]

    def join_groups(ready, ins, outs, whole):
        for n in range(2):
            for b in range(blocks):
                whole[groups(b % 2 * lanes + b // 2), :] = ins[b][n]
            outs[n][...] = whole[...].T

    shape = ((row_count, rhs_count), F32)
    inner_sample, inner_answer = call(
        join_groups, [shape] * 2, parts, [pltpu.VMEM((rhs_count, row_count), F32)]
    )

    def leaf_back(ready, ins, outs):
        outs[0][...] = (ins[chips][...].astype(F32) - chip_total(ins[:chips])).astype(BF16)

    terms[0] = after(terms[0], inner_sample, inner_answer, leaf_sample)
    back = call(leaf_back, ((half, width), BF16), [*terms, leaf_half])
    back_far = across(back, 1, leaves)

    def leaf_last(ready, ins, outs, whole):
        in_order(ins[0], ins[1], whole)
        is_leaf = height() == 0
        outs[0][...] = jnp.where(is_leaf, ins[2][...], ins[3][...])
        ready()
        outs[1][...] = jnp.where(is_leaf, mmt(ins[5][...], whole[...]), ins[4][...])

    sample, answer = call(
        leaf_last,
        [shape] * 2,
        [back, back_far, leaf_sample, inner_sample, inner_answer, inverse_own],
        whole_half,
    )
    return (sample[None], answer[None])


def solution(mesh):
    in_specs = (
        P("lvl", "col", None),
        P("lvl", None, "col", None),
        P("lvl", "col", None),
        P("lvl", None, None, None),
    )
    out_specs = (P("lvl", "col", None), P("lvl", "col", None))
    return jax.shard_map(
        on_device, mesh=mesh, in_specs=in_specs, out_specs=out_specs, check_vma=False
    )
```

```python
import jax
import jax.numpy as jnp
from jax import lax
from jax.experimental import pallas as pl
from jax.experimental.pallas import tpu as pltpu
from jax.sharding import PartitionSpec as P

F32 = jnp.float32
BF16 = jnp.bfloat16


def trailing_ones(node):
    ones = 0
    while node % 2 == 1:
        ones += 1
        node //= 2
    return ones


def child_links(section, members):
    reach = 2 ** (section - 1)
    parents = [node for node in range(members) if trailing_ones(node) == section]
    links = [[(node - reach, node) for node in parents], [(node + reach, node) for node in parents]]
    return [[(a, b) for a, b in side if a < members] for side in links if any(a < members for a, b in side)]


def mm(a, b):
    return jnp.dot(a, b, preferred_element_type=F32)


def mmt(a, b):
    return lax.dot_general(a, b, (((1,), (1,)), ((), ())), preferred_element_type=F32)


def call(body, outs, args, scratch=()):
    single = isinstance(outs, tuple)
    shapes = [outs] if single else outs

    def kernel(*refs):
        middle = len(args) + len(shapes)
        body(refs[: len(args)], refs[len(args) : middle], *refs[middle:])

    moved = sum(a.size * a.dtype.itemsize for a in args)
    result = pl.pallas_call(
        kernel,
        out_shape=[jax.ShapeDtypeStruct(shape, dtype) for shape, dtype in shapes],
        in_specs=[pl.BlockSpec(memory_space=pltpu.VMEM) for _ in args],
        out_specs=[pl.BlockSpec(memory_space=pltpu.VMEM) for _ in shapes],
        scratch_shapes=list(scratch),
        compiler_params=pltpu.CompilerParams(vmem_limit_bytes=24 << 20),
        cost_estimate=pl.CostEstimate(flops=1 << 28, bytes_accessed=moved, transcendentals=0),
    )(*args)
    return result[0] if single else result


def on_device(rhs, panel, inverse_t, pattern):
    members = lax.axis_size("lvl")
    cols = lax.axis_size("col")
    levels = members.bit_length() - 1
    last = levels - 1
    chips = cols // 2
    lanes = 1 << ((chips.bit_length() - 1) // 2)
    row_count, rhs_count = rhs.shape[1:]
    width = inverse_t.shape[2]
    blocks = 2 * lanes
    group = rhs_count // blocks
    half = rhs_count // 2
    levels_of = [trailing_ones(node) for node in range(members)]
    nodes_at = [[node for node in range(members) if levels_of[node] == s] for s in range(levels + 1)]
    leaves = nodes_at[0]
    inner = [node for node in range(members) if levels_of[node] > 0]

    def place():
        at = lax.axis_index("col")
        core, lane = at % 2, at // 2 % lanes
        return at // blocks, lane, core, core * lanes + lane

    def height():
        at, rank = lax.axis_index("lvl"), 0
        for s in range(1, levels + 1):
            rank = rank + ((at + 1) % 2**s == 0).astype(jnp.int32)
        return rank

    def across(x, offset, planes):
        pairs = [(p * cols + c, p * cols + (c ^ offset)) for p in planes for c in range(cols)]
        return lax.ppermute(x, ("lvl", "col"), pairs)

    def along(x, links, offset=0):
        pairs = [(a * cols + c, b * cols + (c ^ offset)) for a, b in links for c in range(cols)]
        return lax.ppermute(x, ("lvl", "col"), pairs)

    def down(links):
        return [(b, a) for a, b in links]

    def after(x, *earlier):
        return lax.optimization_barrier((x, *earlier))[0]

    def over_chips(mine):
        return [mine] + [across(mine, 2 * chip, leaves) for chip in range(1, chips)]

    def over_rows(mine, planes):
        return [mine] + [across(mine, offset, planes) for offset in range(2 * lanes, cols, 2 * lanes)]

    def chip_total(refs):
        parts = []
        for i in range(lanes):
            total = refs[0][i * group : (i + 1) * group, :].astype(F32)
            for chip in range(1, chips):
                k = i ^ (chip % lanes)
                total = total + refs[chip][k * group : (k + 1) * group, :].astype(F32)
            parts.append(total)
        return jnp.concatenate(parts, axis=0)

    def row_total(refs):
        total = refs[0][...].astype(F32)
        for ref in refs[1:]:
            total = total + ref[...].astype(F32)
        return total

    def total_of(parts):
        total = parts[0]
        for part in parts[1:]:
            total = total + part
        return total

    def groups(b):
        return pl.ds(pl.multiple_of((b ^ place()[3]) * group, group), group)

    inverse_own, rhs_own = inverse_t[0], rhs[0]
    chip_rows = len(range(0, cols, 2 * lanes))

    def leaf_first(ins, outs, turned, ordered):
        turned[...] = ins[0][...].T
        for b in range(blocks):
            ordered[b * group : (b + 1) * group, :] = turned[groups(b), :]
        terms = ordered[...].astype(BF16)
        outs[0][...] = mm(terms[:half], ins[1][...]).astype(BF16)
        outs[1][...] = mm(terms[half:], ins[1][...]).astype(BF16)

    keep, give = call(
        leaf_first,
        [((half, width), BF16)] * 2,
        [rhs_own, inverse_own],
        [pltpu.VMEM((rhs_count, row_count), F32)] * 2,
    )
    got = across(give, 1, leaves)

    tiles = pattern.shape[-1]
    tile = width // tiles

    def build(ins, outs):
        pattern_ref, _, rhs_ref, inv_ref, panel_ref = ins
        first_row = lax.axis_index("col") * row_count
        row_ids = lax.broadcasted_iota(jnp.int32, (row_count, tiles), 0) + first_row
        row_tile = lax.broadcasted_iota(jnp.int32, (row_count, tiles), 1)
        row_pick = ((row_ids >= row_tile * tile) & (row_ids < (row_tile + 1) * tile)).astype(F32).astype(BF16)
        col_ids = lax.broadcasted_iota(jnp.int32, (tiles, width), 1)
        col_tile = lax.broadcasted_iota(jnp.int32, (tiles, width), 0)
        col_pick = ((col_ids >= col_tile * tile) & (col_ids < (col_tile + 1) * tile)).astype(F32).astype(BF16)
        masks = []
        for k in range(levels):
            kept = mm(row_pick, pattern_ref[0, k].astype(F32).astype(BF16)).astype(BF16)
            masks.append(mm(kept, col_pick).astype(BF16))
        high = rhs_ref[...].astype(BF16)
        low = (rhs_ref[...] - high.astype(F32)).astype(BF16)
        outs[0][:, levels * width : levels * width + rhs_count] = high
        outs[0][:, levels * width + rhs_count :] = low
        for k in range(levels):
            block = panel_ref[0, k] * masks[k]
            if k == last:
                block = jnp.where(height() == 0, block, inv_ref[...])
            outs[0][:, k * width : (k + 1) * width] = block

    full = levels * width + 2 * rhs_count
    rows_own = call(build, ((row_count, full), BF16), [pattern, give, rhs_own, inverse_own, panel])
    rows_own = after(rows_own, got)
    rows_far = across(rows_own, 1, range(members))
    rows_lanes = [across(rows_own, 2 * i, inner) for i in range(1, lanes)]
    chip_part = (keep.astype(F32) + got.astype(F32)).astype(BF16)
    terms = over_chips(chip_part)

    def factor_of(ref, k):
        return ref[:, k * width : (k + 1) * width]

    def inverse_of(ref):
        return factor_of(ref, last)

    def leaf_push(ins, outs):
        solved = chip_total(ins[:chips]).astype(BF16)
        outs[0][...] = solved
        for k in range(levels):
            for j in range(2):
                product = mmt(solved, factor_of(ins[chips + j], k)).astype(BF16)
                outs[1][k, j] = product

    vector = ((blocks, group, row_count), F32)
    term = ((group, width), BF16)
    leaf_half, pushed = call(
        leaf_push,
        [((half, width), BF16), ((levels, 2, half, row_count), BF16)],
        [*terms, rows_own, rows_far],
    )
    sides = child_links(1, members)
    early = [along(pushed, links) for links in sides]

    samples = {}
    arrived = []
    for section in range(1, levels + 1):
        remain = levels - section
        nodes = nodes_at[section]

        def inner_first(ins, outs):
            came, pair = ins[:-2], ins[-2:]
            own = lax.broadcasted_iota(jnp.int32, (half, rhs_count), 0)
            at = lax.broadcasted_iota(jnp.int32, (half, rhs_count), 1)
            parts = []
            for j in range(2):
                pick = jnp.zeros((half, rhs_count), BF16)
                for i in range(lanes):
                    mine = (own >= i * group) & (own < (i + 1) * group)
                    spot = own - i * group + (i ^ place()[3]) * group
                    pick = jnp.where(mine & (at == spot), 1.0, pick.astype(F32)).astype(BF16)
                rhs_pair = pair[j][:, levels * width :]
                side = mmt(pick, rhs_pair[:, :rhs_count]) + mmt(pick, rhs_pair[:, rhs_count:])
                less = total_of([ref[0, j].astype(F32) for ref in came])
                parts.append(mm((side - less).astype(BF16), inverse_of(pair[j])))
                for k in range(remain):
                    total = total_of([ref[k + 1, j].astype(F32) for ref in came])
                    outs[1][k, j] = total.astype(BF16)
            outs[0][...] = total_of(parts).astype(BF16)

        outs = [((half, width), BF16)] + ([((remain, 2, half, row_count), BF16)] if remain else [])
        own_term, *more = call(inner_first, outs, [*early, rows_own, rows_far])

        def by_lane(ins, outs):
            total = row_total(ins).astype(BF16)
            for i in range(lanes):
                outs[i][...] = total[i * group : (i + 1) * group]

        parts = over_rows(own_term, nodes)
        if remain:
            early = [along(more[0], links) for links in child_links(section + 1, members)]
            parts[0] = after(parts[0], *early)
        own_term, *others = call(by_lane, [term] * lanes, parts)
        terms = [own_term] + [across(others[i - 1], 2 * i, nodes) for i in range(1, lanes)]
        if arrived:

            def inner_second(ins, outs):
                came, rows_of = ins[:-blocks], ins[-blocks:]
                parts = []
                for b in range(blocks):
                    less = total_of([ref[0, b].astype(F32) for ref in came])
                    parts.append(mm(less.astype(BF16), inverse_of(rows_of[b])))
                outs[0][...] = (-total_of(parts)).astype(BF16)

            terms += over_rows(call(inner_second, term, [*arrived, *inner_rows]), nodes)
        count = len(terms)
        if section == 1:
            inner_rows = [rows_own, rows_far]
            for near in rows_lanes:
                inner_rows += [near, across(after(near, own_term), 1, inner)]
            leaf_far = across(after(leaf_half, own_term), 1, leaves)
        if remain:

            def inner_push(ins, outs):
                solved = row_total(ins[:count])
                came, rows_of = ins[count:-blocks], ins[-blocks:]
                outs[0][...] = solved
                short = solved.astype(BF16)
                for k in range(remain):
                    for b in range(blocks):
                        product = mmt(short, factor_of(rows_of[b], k))
                        if came:
                            product = product + total_of([ref[k + 1, b].astype(F32) for ref in came])
                        outs[1][k, b] = product.astype(BF16)

            samples[section], sent = call(
                inner_push,
                [((group, width), F32), ((remain, blocks, group, row_count), BF16)],
                [*terms, *arrived, *inner_rows],
            )
            arrived = [along(sent, links) for links in child_links(section + 1, members)]

    def root_back(ins, outs):
        solved = row_total(ins[:-blocks])
        outs[0][...] = solved
        short = solved.astype(BF16)
        for b in range(blocks):
            answer = mmt(short, inverse_of(ins[b - blocks]))
            outs[1][b] = answer
            outs[2][0, b] = answer.astype(BF16)

    samples[levels], answer, sent = call(
        root_back,
        [((group, width), F32), vector, ((1, blocks, group, row_count), BF16)],
        [*terms, *inner_rows],
    )

    def split_rows(ins, outs):
        rank = height()
        solved = ins[0][...]
        for s in range(2, levels + 1):
            solved = jnp.where(rank == s, ins[s - 1][...], solved)
        high = solved.astype(BF16)
        stacked = jnp.concatenate([high, (solved - high.astype(F32)).astype(BF16)], axis=0)
        row, lane, core, _ = place()
        for b in range(blocks):
            start = (row * blocks + (b ^ (lane * 2 + core))) * row_count
            at = lax.broadcasted_iota(jnp.int32, (row_count, width), 0) + start
            pick = (lax.broadcasted_iota(jnp.int32, (row_count, width), 1) == at).astype(F32).astype(BF16)
            both = mmt(stacked, pick)
            outs[0][b] = both[:group] + both[group:]

    for section in range(levels - 1, 0, -1):
        remain = levels - section
        ancestry = total_of([along(sent, down(links)) for links in child_links(section + 1, members)])

        def adjoint_first(ins, outs):
            parts = []
            for b in range(blocks):
                for k in range(remain):
                    parts.append(mm(ins[0][k, b], factor_of(ins[1 + b], k)))
            outs[0][...] = total_of(parts).astype(BF16)

        own_term = call(adjoint_first, term, [ancestry, *inner_rows])
        terms = over_rows(own_term, nodes_at[section])
        if section == 1:
            order = [after(samples[s], own_term) for s in range(1, levels + 1)]
            sample_rows = call(split_rows, vector, order)

        def inner_back(ins, outs):
            came, ins = ins[:chip_rows], ins[chip_rows:]
            (solved, anc, higher), rows_of = ins[:3], ins[3 : 3 + blocks]
            back = (solved[...] - row_total(came)).astype(BF16)
            rank = height()
            for b in range(blocks):
                mine = mmt(back, inverse_of(rows_of[b]))
                if section > 1:
                    outs[0][b] = jnp.where(rank == section, mine, higher[b])
                    outs[1][0, b] = mine.astype(BF16)
                    for k in range(remain):
                        outs[1][k + 1, b] = anc[k, b]
                else:
                    outs[b // 2][0, b % 2] = mine.astype(BF16)
                    for k in range(remain):
                        outs[b // 2][k + 1, b % 2] = anc[k, b]
                    outs[lanes + b][0] = ins[-1][b]
                    outs[lanes + b][1] = jnp.where(rank == 1, mine, higher[b])

        args = [*terms, samples[section], ancestry, answer, *inner_rows]
        if section > 1:
            answer, sent = call(
                inner_back, [vector, ((remain + 1, blocks, group, row_count), BF16)], args
            )
        else:
            message = ((levels, 2, group, row_count), BF16)
            outs = [message] * lanes + [((2, group, row_count), F32)] * blocks
            results = call(inner_back, outs, [*args, sample_rows])
            sent, results = results[:lanes], results[lanes:]

    arrived = [along(sent[i], down(links), 2 * i) for i in range(lanes) for links in sides]

    def leaf_adjoint(ins, outs):
        came, pair = ins[:-2], ins[-2:]
        parts = []
        for k in range(levels):
            for j in range(2):
                anc = [came[2 * i][k, j] + came[2 * i + 1][k, j] for i in range(lanes)]
                parts.append(mm(jnp.concatenate(anc, axis=0), factor_of(pair[j], k)))
        outs[0][...] = total_of(parts).astype(BF16)

    own_term = call(leaf_adjoint, ((half, width), BF16), [*arrived, rows_own, rows_far])
    terms = over_chips(own_term)

    def in_order(near, far, whole):
        for b in range(blocks):
            source = near if b < lanes else far
            whole[groups(b), :] = source[b % lanes * group : (b % lanes + 1) * group, :]

    def leaf_rows(ins, outs, whole):
        in_order(ins[0], ins[1], whole)
        at = lax.broadcasted_iota(jnp.int32, (row_count, width), 0) + lax.axis_index("col") * row_count
        pick = (lax.broadcasted_iota(jnp.int32, (row_count, width), 1) == at).astype(F32).astype(BF16)
        outs[0][...] = mmt(pick, whole[...])

    whole_half = [pltpu.VMEM((rhs_count, width), BF16)]
    leaf_sample = call(leaf_rows, ((row_count, rhs_count), F32), [leaf_half, leaf_far], whole_half)

    parts = [results[0]] + [across(results[b], b, inner) for b in range(1, blocks)]

    def join_groups(ins, outs, whole):
        for n in range(2):
            for b in range(blocks):
                whole[groups(b % 2 * lanes + b // 2), :] = ins[b][n]
            outs[n][...] = whole[...].T

    shape = ((row_count, rhs_count), F32)
    inner_sample, inner_answer = call(
        join_groups, [shape] * 2, parts, [pltpu.VMEM((rhs_count, row_count), F32)]
    )

    def leaf_back(ins, outs):
        outs[0][...] = (ins[chips][...].astype(F32) - chip_total(ins[:chips])).astype(BF16)

    terms[0] = after(terms[0], inner_sample, inner_answer, leaf_sample)
    back = call(leaf_back, ((half, width), BF16), [*terms, leaf_half])
    back_far = across(back, 1, leaves)

    def leaf_last(ins, outs, whole):
        in_order(ins[0], ins[1], whole)
        is_leaf = height() == 0
        outs[0][...] = jnp.where(is_leaf, ins[2][...], ins[3][...])
        outs[1][...] = jnp.where(is_leaf, mmt(ins[5][...], whole[...]), ins[4][...])

    sample, answer = call(
        leaf_last,
        [shape] * 2,
        [back, back_far, leaf_sample, inner_sample, inner_answer, inverse_own],
        whole_half,
    )
    return (sample[None], answer[None])


def solution(mesh):
    in_specs = (
        P("lvl", "col", None),
        P("lvl", None, "col", None),
        P("lvl", "col", None),
        P("lvl", None, None, None),
    )
    out_specs = (P("lvl", "col", None), P("lvl", "col", None))
    return jax.shard_map(
        on_device, mesh=mesh, in_specs=in_specs, out_specs=out_specs, check_vma=False
    )
```

```python
import jax
import jax.numpy as jnp
from jax import lax
from jax.experimental import pallas as pl
from jax.experimental.pallas import tpu as pltpu
from jax.sharding import PartitionSpec as P

F32 = jnp.float32
BF16 = jnp.bfloat16


def trailing_ones(node):
    ones = 0
    while node % 2 == 1:
        ones += 1
        node //= 2
    return ones


def child_links(section, members):
    reach = 2 ** (section - 1)
    parents = [node for node in range(members) if trailing_ones(node) == section]
    links = [[(node - reach, node) for node in parents], [(node + reach, node) for node in parents]]
    return [[(a, b) for a, b in side if a < members] for side in links if any(a < members for a, b in side)]


def leaf_rounds(members):
    rounds = []
    for leaf in range(0, members, 2):
        node, slot = leaf, 0
        while node != members - 1:
            reach = 2 ** trailing_ones(node)
            node += reach if node // (2 * reach) % 2 == 0 else -reach
            for sends in rounds:
                if all(leaf != a and node != b for a, _, b in sends):
                    break
            else:
                sends = []
                rounds.append(sends)
            sends.append((leaf, slot, node))
            slot += 1
    return rounds


def mm(a, b):
    return jnp.dot(a, b, preferred_element_type=F32)


def mmt(a, b):
    return lax.dot_general(a, b, (((1,), (1,)), ((), ())), preferred_element_type=F32)


def call(body, outs, args, scratch=()):
    single = isinstance(outs, tuple)
    shapes = [outs] if single else outs

    def kernel(*refs):
        middle = len(args) + len(shapes)
        body(refs[: len(args)], refs[len(args) : middle], *refs[middle:])

    moved = sum(a.size * a.dtype.itemsize for a in args)
    result = pl.pallas_call(
        kernel,
        out_shape=[jax.ShapeDtypeStruct(shape, dtype) for shape, dtype in shapes],
        in_specs=[pl.BlockSpec(memory_space=pltpu.VMEM) for _ in args],
        out_specs=[pl.BlockSpec(memory_space=pltpu.VMEM) for _ in shapes],
        scratch_shapes=list(scratch),
        compiler_params=pltpu.CompilerParams(vmem_limit_bytes=24 << 20),
        cost_estimate=pl.CostEstimate(flops=1 << 28, bytes_accessed=moved, transcendentals=0),
    )(*args)
    return result[0] if single else result


def on_device(rhs, panel, inverse_t, pattern):
    members = lax.axis_size("lvl")
    cols = lax.axis_size("col")
    levels = members.bit_length() - 1
    last = levels - 1
    chips = cols // 2
    lanes = 1 << ((chips.bit_length() - 1) // 2)
    row_count, rhs_count = rhs.shape[1:]
    width = inverse_t.shape[2]
    blocks = 2 * lanes
    group = rhs_count // blocks
    half = rhs_count // 2
    levels_of = [trailing_ones(node) for node in range(members)]
    nodes_at = [[node for node in range(members) if levels_of[node] == s] for s in range(levels + 1)]
    leaves = nodes_at[0]
    inner = [node for node in range(members) if levels_of[node] > 0]

    def place():
        at = lax.axis_index("col")
        core, lane = at % 2, at // 2 % lanes
        return at // blocks, lane, core, core * lanes + lane

    def height():
        at, rank = lax.axis_index("lvl"), 0
        for s in range(1, levels + 1):
            rank = rank + ((at + 1) % 2**s == 0).astype(jnp.int32)
        return rank

    def across(x, offset, planes):
        pairs = [(p * cols + c, p * cols + (c ^ offset)) for p in planes for c in range(cols)]
        return lax.ppermute(x, ("lvl", "col"), pairs)

    def along(x, links, offset=0):
        pairs = [(a * cols + c, b * cols + (c ^ offset)) for a, b in links for c in range(cols)]
        return lax.ppermute(x, ("lvl", "col"), pairs)

    def down(links):
        return [(b, a) for a, b in links]

    def after(x, *earlier):
        return lax.optimization_barrier((x, *earlier))[0]

    def over_chips(mine):
        return [mine] + [across(mine, 2 * chip, leaves) for chip in range(1, chips)]

    def over_rows(mine, planes):
        return [mine] + [across(mine, offset, planes) for offset in range(2 * lanes, cols, 2 * lanes)]

    def chip_total(refs):
        parts = []
        for i in range(lanes):
            total = refs[0][i * group : (i + 1) * group, :].astype(F32)
            for chip in range(1, chips):
                k = i ^ (chip % lanes)
                total = total + refs[chip][k * group : (k + 1) * group, :].astype(F32)
            parts.append(total)
        return jnp.concatenate(parts, axis=0)

    def row_total(refs):
        total = refs[0][...].astype(F32)
        for ref in refs[1:]:
            total = total + ref[...].astype(F32)
        return total

    def total_of(parts):
        total = parts[0]
        for part in parts[1:]:
            total = total + part
        return total

    def groups(b):
        return pl.ds(pl.multiple_of((b ^ place()[3]) * group, group), group)

    inverse_own, rhs_own = inverse_t[0], rhs[0]
    chip_rows = len(range(0, cols, 2 * lanes))

    def leaf_first(ins, outs, turned, ordered):
        turned[...] = ins[0][...].T
        for b in range(blocks):
            ordered[b * group : (b + 1) * group, :] = turned[groups(b), :]
        terms = ordered[...].astype(BF16)
        outs[0][...] = mm(terms[:half], ins[1][...]).astype(BF16)
        outs[1][...] = mm(terms[half:], ins[1][...]).astype(BF16)

    keep, give = call(
        leaf_first,
        [((half, width), BF16)] * 2,
        [rhs_own, inverse_own],
        [pltpu.VMEM((rhs_count, row_count), F32)] * 2,
    )
    got = across(give, 1, leaves)

    tiles = pattern.shape[-1]
    tile = width // tiles

    def build(ins, outs):
        pattern_ref, _, rhs_ref, inv_ref, panel_ref = ins
        first_row = lax.axis_index("col") * row_count
        row_ids = lax.broadcasted_iota(jnp.int32, (row_count, tiles), 0) + first_row
        row_tile = lax.broadcasted_iota(jnp.int32, (row_count, tiles), 1)
        row_pick = ((row_ids >= row_tile * tile) & (row_ids < (row_tile + 1) * tile)).astype(F32).astype(BF16)
        col_ids = lax.broadcasted_iota(jnp.int32, (tiles, width), 1)
        col_tile = lax.broadcasted_iota(jnp.int32, (tiles, width), 0)
        col_pick = ((col_ids >= col_tile * tile) & (col_ids < (col_tile + 1) * tile)).astype(F32).astype(BF16)
        masks = []
        for k in range(levels):
            kept = mm(row_pick, pattern_ref[0, k].astype(F32).astype(BF16)).astype(BF16)
            masks.append(mm(kept, col_pick).astype(BF16))
        high = rhs_ref[...].astype(BF16)
        low = (rhs_ref[...] - high.astype(F32)).astype(BF16)
        outs[0][:, levels * width : levels * width + rhs_count] = high
        outs[0][:, levels * width + rhs_count :] = low
        for k in range(levels):
            block = panel_ref[0, k] * masks[k]
            if k == last:
                block = jnp.where(height() == 0, block, inv_ref[...])
            outs[0][:, k * width : (k + 1) * width] = block
            outs[1][:, k * width : (k + 1) * width] = block

    full = levels * width + 2 * rhs_count
    rows_own, rows_sent = call(
        build,
        [((row_count, full), BF16), ((row_count, levels * width), BF16)],
        [pattern, give, rhs_own, inverse_own, panel],
    )
    rows_own, rows_sent = after((rows_own, rows_sent), got)
    rows_far = across(rows_own, 1, range(members))
    rows_lanes = [across(rows_sent, 2 * i, inner) for i in range(1, lanes)]
    chip_part = (keep.astype(F32) + got.astype(F32)).astype(BF16)
    terms = over_chips(chip_part)

    def factor_of(ref, k):
        return ref[:, k * width : (k + 1) * width]

    def inverse_of(ref):
        return factor_of(ref, last)

    rounds = leaf_rounds(members)

    def leaf_push(ins, outs):
        solved = chip_total(ins[:chips]).astype(BF16)
        outs[0][...] = solved
        for n, sends in enumerate(rounds):
            slot = total_of([jnp.where(lax.axis_index("lvl") == leaf, k, 0) for leaf, k, _ in sends])
            columns = pl.ds(pl.multiple_of(slot * width, width), width)
            for j in range(2):
                outs[1 + n][j] = mmt(solved, ins[chips + j][:, columns]).astype(BF16)

    vector = ((blocks, group, row_count), F32)
    term = ((group, width), BF16)
    leaf_half, *pushed = call(
        leaf_push,
        [((half, width), BF16)] + [((2, half, row_count), BF16)] * len(rounds),
        [*terms, rows_own, rows_far],
    )
    early = [along(sent, [(a, b) for a, _, b in sends]) for sent, sends in zip(pushed, rounds)]

    def inner_first(ins, outs):
        came, pair = ins[:-2], ins[-2:]
        own = lax.broadcasted_iota(jnp.int32, (half, rhs_count), 0)
        at = lax.broadcasted_iota(jnp.int32, (half, rhs_count), 1)
        pick = jnp.zeros((half, rhs_count), F32)
        for i in range(lanes):
            mine = (own >= i * group) & (own < (i + 1) * group)
            spot = own - i * group + (i ^ place()[3]) * group
            pick = jnp.where(mine & (at == spot), 1.0, pick)
        pick = pick.astype(BF16)
        parts = []
        for j in range(2):
            rhs_pair = pair[j][:, levels * width :]
            side = mmt(pick, rhs_pair[:, :rhs_count]) + mmt(pick, rhs_pair[:, rhs_count:])
            less = total_of([ref[j].astype(F32) for ref in came])
            parts.append(mm((side - less).astype(BF16), inverse_of(pair[j])))
        outs[0][...] = total_of(parts).astype(BF16)

    def by_lane(ins, outs):
        total = row_total(ins).astype(BF16)
        for i in range(lanes):
            outs[i][...] = total[i * group : (i + 1) * group]

    own_term = call(inner_first, ((half, width), BF16), [*early, rows_own, rows_far])
    first_term, *others = call(by_lane, [term] * lanes, over_rows(own_term, inner))
    first_terms = [first_term] + [across(others[i - 1], 2 * i, inner) for i in range(1, lanes)]
    inner_rows = [rows_own, rows_far]
    for near in rows_lanes:
        inner_rows += [near, across(after(near, first_term), 1, inner)]
    leaf_far = across(after(leaf_half, first_term), 1, leaves)

    samples = {}
    arrived = []
    for section in range(1, levels + 1):
        remain = levels - section
        nodes = nodes_at[section]
        terms = list(first_terms)
        if arrived:

            def inner_second(ins, outs):
                came, rows_of = ins[:-blocks], ins[-blocks:]
                parts = []
                for b in range(blocks):
                    less = total_of([ref[0, b].astype(F32) for ref in came])
                    parts.append(mm(less.astype(BF16), inverse_of(rows_of[b])))
                outs[0][...] = (-total_of(parts)).astype(BF16)

            terms += over_rows(call(inner_second, term, [*arrived, *inner_rows]), nodes)
        count = len(terms)
        if remain:

            def inner_push(ins, outs):
                solved = row_total(ins[:count])
                came, rows_of = ins[count:-blocks], ins[-blocks:]
                outs[0][...] = solved
                short = solved.astype(BF16)
                for k in range(remain):
                    for b in range(blocks):
                        product = mmt(short, factor_of(rows_of[b], k))
                        if came:
                            product = product + total_of([ref[k + 1, b].astype(F32) for ref in came])
                        outs[1][k, b] = product.astype(BF16)

            samples[section], sent = call(
                inner_push,
                [((group, width), F32), ((remain, blocks, group, row_count), BF16)],
                [*terms, *arrived, *inner_rows],
            )
            arrived = [along(sent, links) for links in child_links(section + 1, members)]

    def root_back(ins, outs):
        solved = row_total(ins[:-blocks])
        outs[0][...] = solved
        short = solved.astype(BF16)
        for b in range(blocks):
            answer = mmt(short, inverse_of(ins[b - blocks]))
            outs[1][b] = answer
            outs[2][0, b] = answer.astype(BF16)

    samples[levels], answer, sent = call(
        root_back,
        [((group, width), F32), vector, ((1, blocks, group, row_count), BF16)],
        [*terms, *inner_rows],
    )

    leaf_rows_of = [rows_own, rows_far]
    leaf_lanes = [across(after(rows_sent, sent), 2 * i, leaves) for i in range(1, lanes)]

    def split_rows(ins, outs):
        rank = height()
        solved = ins[0][...]
        for s in range(2, levels + 1):
            solved = jnp.where(rank == s, ins[s - 1][...], solved)
        high = solved.astype(BF16)
        stacked = jnp.concatenate([high, (solved - high.astype(F32)).astype(BF16)], axis=0)
        row, lane, core, _ = place()
        for b in range(blocks):
            start = (row * blocks + (b ^ (lane * 2 + core))) * row_count
            at = lax.broadcasted_iota(jnp.int32, (row_count, width), 0) + start
            pick = (lax.broadcasted_iota(jnp.int32, (row_count, width), 1) == at).astype(F32).astype(BF16)
            both = mmt(stacked, pick)
            outs[0][b] = both[:group] + both[group:]

    for section in range(levels - 1, 0, -1):
        remain = levels - section
        ancestry = total_of([along(sent, down(links)) for links in child_links(section + 1, members)])

        def adjoint_first(ins, outs):
            parts = []
            for b in range(blocks):
                for k in range(remain):
                    parts.append(mm(ins[0][k, b], factor_of(ins[1 + b], k)))
            outs[0][...] = total_of(parts).astype(BF16)

        own_term = call(adjoint_first, term, [ancestry, *inner_rows])
        terms = over_rows(own_term, nodes_at[section])
        if section == 1:
            for near in leaf_lanes:
                leaf_rows_of += [near, across(after(near, own_term), 1, leaves)]
            order = [after(samples[s], own_term) for s in range(1, levels + 1)]
            sample_rows = call(split_rows, vector, order)

        def inner_back(ins, outs):
            came, ins = ins[:chip_rows], ins[chip_rows:]
            (solved, anc, higher), rows_of = ins[:3], ins[3 : 3 + blocks]
            back = (solved[...] - row_total(came)).astype(BF16)
            rank = height()
            for b in range(blocks):
                mine = mmt(back, inverse_of(rows_of[b]))
                outs[0][0, b] = mine.astype(BF16)
                for k in range(remain):
                    outs[0][k + 1, b] = anc[k, b]
                chosen = jnp.where(rank == section, mine, higher[b])
                if section == 1:
                    outs[1 + b][0] = ins[-1][b]
                    outs[1 + b][1] = chosen
                else:
                    outs[1][b] = chosen

        args = [*terms, samples[section], ancestry, answer, *inner_rows]
        outs = [((remain + 1, blocks, group, row_count), BF16)]
        if section == 1:
            args, outs = [*args, sample_rows], outs + [((2, group, row_count), F32)] * blocks
        else:
            outs = [*outs, vector]
        sent, *results = call(inner_back, outs, args)
        answer = results[0]

    ancestry = [along(sent, down(links)) for links in child_links(1, members)]

    def leaf_adjoint(ins, outs):
        came, rows_of = ins[:-blocks], ins[-blocks:]
        parts = []
        for b in range(blocks):
            for k in range(levels):
                parts.append(mm(total_of([ref[k, b] for ref in came]), factor_of(rows_of[b], k)))
        outs[0][...] = total_of(parts).astype(BF16)

    own_term = call(leaf_adjoint, term, [*ancestry, *leaf_rows_of])
    terms = over_rows(own_term, leaves)

    def in_order(near, far, whole):
        for b in range(blocks):
            source = near if b < lanes else far
            whole[groups(b), :] = source[b % lanes * group : (b % lanes + 1) * group, :]

    def leaf_rows(ins, outs, whole):
        in_order(ins[0], ins[1], whole)
        at = lax.broadcasted_iota(jnp.int32, (row_count, width), 0) + lax.axis_index("col") * row_count
        pick = (lax.broadcasted_iota(jnp.int32, (row_count, width), 1) == at).astype(F32).astype(BF16)
        outs[0][...] = mmt(pick, whole[...])

    whole_half = [pltpu.VMEM((rhs_count, width), BF16)]
    leaf_sample = call(leaf_rows, ((row_count, rhs_count), F32), [leaf_half, leaf_far], whole_half)

    parts = [results[0]] + [across(results[b], b, inner) for b in range(1, blocks)]

    def join_groups(ins, outs, whole):
        for n in range(2):
            for b in range(blocks):
                whole[groups(b % 2 * lanes + b // 2), :] = ins[b][n]
            outs[n][...] = whole[...].T

    shape = ((row_count, rhs_count), F32)
    inner_sample, inner_answer = call(
        join_groups, [shape] * 2, parts, [pltpu.VMEM((rhs_count, row_count), F32)]
    )

    def leaf_back(ins, outs):
        mine = ins[0][:group, :].astype(F32)
        outs[0][...] = (mine - row_total(ins[1:])).astype(BF16)

    terms[0] = after(terms[0], inner_sample, inner_answer, leaf_sample)
    back = call(leaf_back, term, [leaf_half, *terms])
    backs = [back] + [across(back, b, leaves) for b in range(1, blocks)]

    def leaf_last(ins, outs, whole):
        leaf_ref, inner_ref, answer_ref, inv_ref = ins[blocks:]
        for b in range(blocks):
            whole[groups(b % 2 * lanes + b // 2), :] = ins[b][...]
        is_leaf = height() == 0
        outs[0][...] = jnp.where(is_leaf, leaf_ref[...], inner_ref[...])
        outs[1][...] = jnp.where(is_leaf, mmt(inv_ref[...], whole[...]), answer_ref[...])

    sample, answer = call(
        leaf_last,
        [shape] * 2,
        [*backs, leaf_sample, inner_sample, inner_answer, inverse_own],
        whole_half,
    )
    return (sample[None], answer[None])


def solution(mesh):
    in_specs = (
        P("lvl", "col", None),
        P("lvl", None, "col", None),
        P("lvl", "col", None),
        P("lvl", None, None, None),
    )
    out_specs = (P("lvl", "col", None), P("lvl", "col", None))
    return jax.shard_map(
        on_device, mesh=mesh, in_specs=in_specs, out_specs=out_specs, check_vma=False
    )
```

```python
import jax
import jax.numpy as jnp
from jax import lax
from jax.experimental import pallas as pl
from jax.experimental.pallas import tpu as pltpu
from jax.sharding import PartitionSpec as P

F32 = jnp.float32
BF16 = jnp.bfloat16


def trailing_ones(node):
    ones = 0
    while node % 2 == 1:
        ones += 1
        node //= 2
    return ones


def child_links(section, members):
    reach = 2 ** (section - 1)
    parents = [node for node in range(members) if trailing_ones(node) == section]
    links = [[(node - reach, node) for node in parents], [(node + reach, node) for node in parents]]
    return [[(a, b) for a, b in side if a < members] for side in links if any(a < members for a, b in side)]


def leaf_rounds(members):
    rounds = []
    for leaf in range(0, members, 2):
        node, slot = leaf, 0
        while node != members - 1:
            reach = 2 ** trailing_ones(node)
            node += reach if node // (2 * reach) % 2 == 0 else -reach
            for sends in rounds:
                if all(leaf != a and node != b for a, _, b in sends):
                    break
            else:
                sends = []
                rounds.append(sends)
            sends.append((leaf, slot, node))
            slot += 1
    return rounds


def mm(a, b):
    return jnp.dot(a, b, preferred_element_type=F32)


def mmt(a, b):
    return lax.dot_general(a, b, (((1,), (1,)), ((), ())), preferred_element_type=F32)


def call(body, outs, args, scratch=()):
    single = isinstance(outs, tuple)
    shapes = [outs] if single else outs

    def kernel(*refs):
        middle = len(args) + len(shapes)
        body(refs[: len(args)], refs[len(args) : middle], *refs[middle:])

    moved = sum(a.size * a.dtype.itemsize for a in args)
    result = pl.pallas_call(
        kernel,
        out_shape=[jax.ShapeDtypeStruct(shape, dtype) for shape, dtype in shapes],
        in_specs=[pl.BlockSpec(memory_space=pltpu.VMEM) for _ in args],
        out_specs=[pl.BlockSpec(memory_space=pltpu.VMEM) for _ in shapes],
        scratch_shapes=list(scratch),
        compiler_params=pltpu.CompilerParams(vmem_limit_bytes=24 << 20),
        cost_estimate=pl.CostEstimate(flops=1 << 28, bytes_accessed=moved, transcendentals=0),
    )(*args)
    return result[0] if single else result


def on_device(rhs, panel, inverse_t, pattern):
    members = lax.axis_size("lvl")
    cols = lax.axis_size("col")
    levels = members.bit_length() - 1
    last = levels - 1
    chips = cols // 2
    lanes = 1 << ((chips.bit_length() - 1) // 2)
    row_count, rhs_count = rhs.shape[1:]
    width = inverse_t.shape[2]
    blocks = 2 * lanes
    group = rhs_count // blocks
    half = rhs_count // 2
    levels_of = [trailing_ones(node) for node in range(members)]
    nodes_at = [[node for node in range(members) if levels_of[node] == s] for s in range(levels + 1)]
    leaves = nodes_at[0]
    inner = [node for node in range(members) if levels_of[node] > 0]

    def place():
        at = lax.axis_index("col")
        core, lane = at % 2, at // 2 % lanes
        return at // blocks, lane, core, core * lanes + lane

    def height():
        at, rank = lax.axis_index("lvl"), 0
        for s in range(1, levels + 1):
            rank = rank + ((at + 1) % 2**s == 0).astype(jnp.int32)
        return rank

    def permute(x, moves):
        pairs = []
        for plane in range(members):
            target, offset = moves.get(plane, (plane, 1))
            pairs += [(plane * cols + c, target * cols + (c ^ offset)) for c in range(cols)]
        return lax.ppermute(x, ("lvl", "col"), pairs)

    def across(x, offset, planes):
        return permute(x, {plane: (plane, offset) for plane in planes})

    def along(x, links, offset=0):
        moves = {}
        for a, b in links:
            moves[a], moves[b] = (b, offset), (a, offset)
        return permute(x, moves)

    def from_parent(left, right, section):
        return jnp.where(lax.axis_index("lvl") // 2**section % 2 == 0, left, right)

    def down(links):
        return [(b, a) for a, b in links]

    def after(x, *earlier):
        return lax.optimization_barrier((x, *earlier))[0]

    def over_chips(mine):
        return [mine] + [across(mine, 2 * chip, leaves) for chip in range(1, chips)]

    def over_rows(mine, planes):
        return [mine] + [across(mine, offset, planes) for offset in range(2 * lanes, cols, 2 * lanes)]

    def chip_total(refs):
        parts = []
        for i in range(lanes):
            total = refs[0][i * group : (i + 1) * group, :].astype(F32)
            for chip in range(1, chips):
                k = i ^ (chip % lanes)
                total = total + refs[chip][k * group : (k + 1) * group, :].astype(F32)
            parts.append(total)
        return jnp.concatenate(parts, axis=0)

    def row_total(refs):
        total = refs[0][...].astype(F32)
        for ref in refs[1:]:
            total = total + ref[...].astype(F32)
        return total

    def total_of(parts):
        total = parts[0]
        for part in parts[1:]:
            total = total + part
        return total

    def span(b):
        return slice(b * row_count, (b + 1) * row_count)

    def groups(b):
        return pl.ds(pl.multiple_of((b ^ place()[3]) * group, group), group)

    inverse_own, rhs_own = inverse_t[0], rhs[0]
    chip_rows = len(range(0, cols, 2 * lanes))

    def leaf_first(ins, outs, turned, ordered):
        turned[...] = ins[0][...].T
        for b in range(blocks):
            ordered[b * group : (b + 1) * group, :] = turned[groups(b), :]
        terms = ordered[...].astype(BF16)
        outs[0][...] = mm(terms[:half], ins[1][...]).astype(BF16)
        outs[1][...] = mm(terms[half:], ins[1][...]).astype(BF16)

    keep, give = call(
        leaf_first,
        [((half, width), BF16)] * 2,
        [rhs_own, inverse_own],
        [pltpu.VMEM((rhs_count, row_count), F32)] * 2,
    )
    got = across(give, 1, leaves)

    tiles = pattern.shape[-1]
    tile = width // tiles

    def build(ins, outs):
        pattern_ref, _, rhs_ref, inv_ref, panel_ref = ins
        first_row = lax.axis_index("col") * row_count
        row_ids = lax.broadcasted_iota(jnp.int32, (row_count, tiles), 0) + first_row
        row_tile = lax.broadcasted_iota(jnp.int32, (row_count, tiles), 1)
        row_pick = ((row_ids >= row_tile * tile) & (row_ids < (row_tile + 1) * tile)).astype(F32).astype(BF16)
        col_ids = lax.broadcasted_iota(jnp.int32, (tiles, width), 1)
        col_tile = lax.broadcasted_iota(jnp.int32, (tiles, width), 0)
        col_pick = ((col_ids >= col_tile * tile) & (col_ids < (col_tile + 1) * tile)).astype(F32).astype(BF16)
        masks = []
        for k in range(levels):
            kept = mm(row_pick, pattern_ref[0, k].astype(F32).astype(BF16)).astype(BF16)
            masks.append(mm(kept, col_pick).astype(BF16))
        high = rhs_ref[...].astype(BF16)
        low = (rhs_ref[...] - high.astype(F32)).astype(BF16)
        outs[0][:, levels * width : levels * width + rhs_count] = high
        outs[0][:, levels * width + rhs_count :] = low
        for k in range(levels):
            block = panel_ref[0, k] * masks[k]
            if k == last:
                block = jnp.where(height() == 0, block, inv_ref[...])
            outs[0][:, k * width : (k + 1) * width] = block
            outs[1][:, k * width : (k + 1) * width] = block

    full = levels * width + 2 * rhs_count
    rows_own, rows_sent = call(
        build,
        [((row_count, full), BF16), ((row_count, levels * width), BF16)],
        [pattern, give, rhs_own, inverse_own, panel],
    )
    rows_own, rows_sent = after((rows_own, rows_sent), got)
    rows_far = across(rows_own, 1, range(members))
    rows_lanes = [across(rows_sent, 2 * i, inner) for i in range(1, lanes)]
    chip_part = (keep.astype(F32) + got.astype(F32)).astype(BF16)
    terms = over_chips(chip_part)

    def factor_of(ref, k):
        return ref[:, k * width : (k + 1) * width]

    def inverse_of(ref):
        return factor_of(ref, last)

    rounds = leaf_rounds(members)

    def leaf_push(ins, outs):
        solved = chip_total(ins[:chips]).astype(BF16)
        outs[0][...] = solved
        for n, sends in enumerate(rounds):
            slot = total_of([jnp.where(lax.axis_index("lvl") == leaf, k, 0) for leaf, k, _ in sends])
            columns = pl.ds(pl.multiple_of(slot * width, width), width)
            for j in range(2):
                outs[1 + n][:, span(j)] = mmt(solved, ins[chips + j][:, columns]).astype(BF16)

    vector = ((blocks, group, row_count), F32)
    term = ((group, width), BF16)
    leaf_half, *pushed = call(
        leaf_push,
        [((half, width), BF16)] + [((half, 2 * row_count), BF16)] * len(rounds),
        [*terms, rows_own, rows_far],
    )
    early = [along(sent, [(a, b) for a, _, b in sends]) for sent, sends in zip(pushed, rounds)]

    def heard(n, part):
        targets = [b for _, _, b in rounds[n]]
        if len(targets) == len(inner):
            return part
        here = total_of([(lax.axis_index("lvl") == b).astype(jnp.int32) for b in targets]) > 0
        return jnp.where(here, part, 0.0)

    def inner_first(ins, outs):
        came, pair = ins[:-2], ins[-2:]
        own = lax.broadcasted_iota(jnp.int32, (half, rhs_count), 0)
        at = lax.broadcasted_iota(jnp.int32, (half, rhs_count), 1)
        pick = jnp.zeros((half, rhs_count), F32)
        for i in range(lanes):
            mine = (own >= i * group) & (own < (i + 1) * group)
            spot = own - i * group + (i ^ place()[3]) * group
            pick = jnp.where(mine & (at == spot), 1.0, pick)
        pick = pick.astype(BF16)
        parts = []
        for j in range(2):
            rhs_pair = pair[j][:, levels * width :]
            side = mmt(pick, rhs_pair[:, :rhs_count]) + mmt(pick, rhs_pair[:, rhs_count:])
            less = total_of([heard(n, ref[:, span(j)].astype(F32)) for n, ref in enumerate(came)])
            parts.append(mm((side - less).astype(BF16), inverse_of(pair[j])))
        outs[0][...] = total_of(parts).astype(BF16)

    def by_lane(ins, outs):
        total = row_total(ins).astype(BF16)
        for i in range(lanes):
            outs[i][...] = total[i * group : (i + 1) * group]

    own_term = call(inner_first, ((half, width), BF16), [*early, rows_own, rows_far])
    first_term, *others = call(by_lane, [term] * lanes, over_rows(own_term, inner))
    first_terms = [first_term] + [across(others[i - 1], 2 * i, inner) for i in range(1, lanes)]
    inner_rows = [rows_own, rows_far]
    for near in rows_lanes:
        inner_rows += [near, across(after(near, first_term), 1, inner)]
    leaf_far = across(after(leaf_half, first_term), 1, leaves)

    samples = {}
    arrived = []
    for section in range(1, levels + 1):
        remain = levels - section
        nodes = nodes_at[section]
        terms = list(first_terms)
        if arrived:

            def inner_second(ins, outs):
                came, rows_of = ins[:-blocks], ins[-blocks:]
                parts = []
                for b in range(blocks):
                    less = total_of([ref[0, :, span(b)].astype(F32) for ref in came])
                    parts.append(mm(less.astype(BF16), inverse_of(rows_of[b])))
                outs[0][...] = (-total_of(parts)).astype(BF16)

            terms += over_rows(call(inner_second, term, [*arrived, *inner_rows]), nodes)
        count = len(terms)
        if remain:

            def inner_push(ins, outs):
                solved = row_total(ins[:count])
                came, rows_of = ins[count:-blocks], ins[-blocks:]
                outs[0][...] = solved
                short = solved.astype(BF16)
                for k in range(remain):
                    for b in range(blocks):
                        product = mmt(short, factor_of(rows_of[b], k))
                        if came:
                            product = product + total_of([ref[k + 1, :, span(b)].astype(F32) for ref in came])
                        outs[1][k, :, span(b)] = product.astype(BF16)

            samples[section], sent = call(
                inner_push,
                [((group, width), F32), ((remain, group, blocks * row_count), BF16)],
                [*terms, *arrived, *inner_rows],
            )
            arrived = [along(sent, links) for links in child_links(section + 1, members)]

    def root_back(ins, outs):
        solved = row_total(ins[:-blocks])
        outs[0][...] = solved
        short = solved.astype(BF16)
        for b in range(blocks):
            answer = mmt(short, inverse_of(ins[b - blocks]))
            outs[1][b] = answer
            outs[2][0, :, span(b)] = answer.astype(BF16)

    samples[levels], answer, sent = call(
        root_back,
        [((group, width), F32), vector, ((1, group, blocks * row_count), BF16)],
        [*terms, *inner_rows],
    )

    leaf_rows_of = [rows_own, rows_far]
    leaf_lanes = [across(after(rows_sent, sent), 2 * i, leaves) for i in range(1, lanes)]

    def split_rows(ins, outs):
        rank = height()
        solved = ins[0][...]
        for s in range(2, levels + 1):
            solved = jnp.where(rank == s, ins[s - 1][...], solved)
        high = solved.astype(BF16)
        stacked = jnp.concatenate([high, (solved - high.astype(F32)).astype(BF16)], axis=0)
        row, lane, core, _ = place()
        for b in range(blocks):
            start = (row * blocks + (b ^ (lane * 2 + core))) * row_count
            at = lax.broadcasted_iota(jnp.int32, (row_count, width), 0) + start
            pick = (lax.broadcasted_iota(jnp.int32, (row_count, width), 1) == at).astype(F32).astype(BF16)
            both = mmt(stacked, pick)
            outs[0][b] = both[:group] + both[group:]

    for section in range(levels - 1, 0, -1):
        remain = levels - section
        ancestry = [along(sent, down(links)) for links in child_links(section + 1, members)]
        ancestry = ancestry[0] if len(ancestry) == 1 else from_parent(*ancestry, section + 1)

        def adjoint_first(ins, outs):
            parts = []
            for b in range(blocks):
                for k in range(remain):
                    parts.append(mm(ins[0][k, :, span(b)], factor_of(ins[1 + b], k)))
            outs[0][...] = total_of(parts).astype(BF16)

        own_term = call(adjoint_first, term, [ancestry, *inner_rows])
        terms = over_rows(own_term, nodes_at[section])
        if section == 1:
            for near in leaf_lanes:
                leaf_rows_of += [near, across(after(near, own_term), 1, leaves)]
            order = [after(samples[s], own_term) for s in range(1, levels + 1)]
            sample_rows = call(split_rows, vector, order)

        def inner_back(ins, outs):
            came, ins = ins[:chip_rows], ins[chip_rows:]
            (solved, anc, higher), rows_of = ins[:3], ins[3 : 3 + blocks]
            back = (solved[...] - row_total(came)).astype(BF16)
            rank = height()
            outs[0][1:] = anc[...]
            for b in range(blocks):
                mine = mmt(back, inverse_of(rows_of[b]))
                outs[0][0, :, span(b)] = mine.astype(BF16)
                chosen = jnp.where(rank == section, mine, higher[b])
                if section == 1:
                    outs[1 + b][0] = ins[-1][b]
                    outs[1 + b][1] = chosen
                else:
                    outs[1][b] = chosen

        args = [*terms, samples[section], ancestry, answer, *inner_rows]
        outs = [((remain + 1, group, blocks * row_count), BF16)]
        if section == 1:
            args, outs = [*args, sample_rows], outs + [((2, group, row_count), F32)] * blocks
        else:
            outs = [*outs, vector]
        sent, *results = call(inner_back, outs, args)
        answer = results[0]

    ancestry = [along(sent, down(links)) for links in child_links(1, members)]

    def leaf_adjoint(ins, outs):
        came, rows_of = ins[:-blocks], ins[-blocks:]
        parts = []
        for b in range(blocks):
            for k in range(levels):
                parts.append(mm(from_parent(*[ref[k, :, span(b)] for ref in came], 1), factor_of(rows_of[b], k)))
        outs[0][...] = total_of(parts).astype(BF16)

    own_term = call(leaf_adjoint, term, [*ancestry, *leaf_rows_of])
    terms = over_rows(own_term, leaves)

    def in_order(near, far, whole):
        for b in range(blocks):
            source = near if b < lanes else far
            whole[groups(b), :] = source[b % lanes * group : (b % lanes + 1) * group, :]

    def leaf_rows(ins, outs, whole):
        in_order(ins[0], ins[1], whole)
        at = lax.broadcasted_iota(jnp.int32, (row_count, width), 0) + lax.axis_index("col") * row_count
        pick = (lax.broadcasted_iota(jnp.int32, (row_count, width), 1) == at).astype(F32).astype(BF16)
        outs[0][...] = mmt(pick, whole[...])

    whole_half = [pltpu.VMEM((rhs_count, width), BF16)]
    leaf_sample = call(leaf_rows, ((row_count, rhs_count), F32), [leaf_half, leaf_far], whole_half)

    parts = [results[0]] + [across(results[b], b, inner) for b in range(1, blocks)]

    def join_groups(ins, outs, whole):
        for n in range(2):
            for b in range(blocks):
                whole[groups(b % 2 * lanes + b // 2), :] = ins[b][n]
            outs[n][...] = whole[...].T

    shape = ((row_count, rhs_count), F32)
    inner_sample, inner_answer = call(
        join_groups, [shape] * 2, parts, [pltpu.VMEM((rhs_count, row_count), F32)]
    )

    def leaf_back(ins, outs):
        mine = ins[0][:group, :].astype(F32)
        outs[0][...] = (mine - row_total(ins[1:])).astype(BF16)

    terms[0] = after(terms[0], inner_sample, inner_answer, leaf_sample)
    back = call(leaf_back, term, [leaf_half, *terms])
    backs = [back] + [across(back, b, leaves) for b in range(1, blocks)]

    def leaf_last(ins, outs, whole):
        leaf_ref, inner_ref, answer_ref, inv_ref = ins[blocks:]
        for b in range(blocks):
            whole[groups(b % 2 * lanes + b // 2), :] = ins[b][...]
        is_leaf = height() == 0
        outs[0][...] = jnp.where(is_leaf, leaf_ref[...], inner_ref[...])
        outs[1][...] = jnp.where(is_leaf, mmt(inv_ref[...], whole[...]), answer_ref[...])

    sample, answer = call(
        leaf_last,
        [shape] * 2,
        [*backs, leaf_sample, inner_sample, inner_answer, inverse_own],
        whole_half,
    )
    return (sample[None], answer[None])


def solution(mesh):
    in_specs = (
        P("lvl", "col", None),
        P("lvl", None, "col", None),
        P("lvl", "col", None),
        P("lvl", None, None, None),
    )
    out_specs = (P("lvl", "col", None), P("lvl", "col", None))
    return jax.shard_map(
        on_device, mesh=mesh, in_specs=in_specs, out_specs=out_specs, check_vma=False
    )
```

```python
import jax
import jax.numpy as jnp
from jax import lax
from jax.experimental import pallas as pl
from jax.experimental.pallas import tpu as pltpu
from jax.sharding import PartitionSpec as P

F32 = jnp.float32
BF16 = jnp.bfloat16


def trailing_ones(node):
    ones = 0
    while node % 2 == 1:
        ones += 1
        node //= 2
    return ones


def child_links(section, members):
    reach = 2 ** (section - 1)
    parents = [node for node in range(members) if trailing_ones(node) == section]
    links = [[(node - reach, node) for node in parents], [(node + reach, node) for node in parents]]
    return [[(a, b) for a, b in side if a < members] for side in links if any(a < members for a, b in side)]


def leaf_rounds(members):
    rounds = []
    for leaf in range(0, members, 2):
        node, slot = leaf, 0
        while node != members - 1:
            reach = 2 ** trailing_ones(node)
            node += reach if node // (2 * reach) % 2 == 0 else -reach
            for sends in rounds:
                if all(leaf != a and node != b for a, _, b in sends):
                    break
            else:
                sends = []
                rounds.append(sends)
            sends.append((leaf, slot, node))
            slot += 1
    return rounds


def mm(a, b):
    return jnp.dot(a, b, preferred_element_type=F32)


def mmt(a, b):
    return lax.dot_general(a, b, (((1,), (1,)), ((), ())), preferred_element_type=F32)


def call(body, outs, args, scratch=()):
    single = isinstance(outs, tuple)
    shapes = [outs] if single else outs

    def kernel(*refs):
        middle = len(args) + len(shapes)
        body(refs[: len(args)], refs[len(args) : middle], *refs[middle:])

    moved = sum(a.size * a.dtype.itemsize for a in args)
    result = pl.pallas_call(
        kernel,
        out_shape=[jax.ShapeDtypeStruct(shape, dtype) for shape, dtype in shapes],
        in_specs=[pl.BlockSpec(memory_space=pltpu.VMEM) for _ in args],
        out_specs=[pl.BlockSpec(memory_space=pltpu.VMEM) for _ in shapes],
        scratch_shapes=list(scratch),
        compiler_params=pltpu.CompilerParams(vmem_limit_bytes=24 << 20),
        cost_estimate=pl.CostEstimate(flops=1 << 28, bytes_accessed=moved, transcendentals=0),
    )(*args)
    return result[0] if single else result


def on_device(rhs, panel, inverse_t, pattern):
    members = lax.axis_size("lvl")
    cols = lax.axis_size("col")
    levels = members.bit_length() - 1
    last = levels - 1
    chips = cols // 2
    lanes = 1 << ((chips.bit_length() - 1) // 2)
    row_count, rhs_count = rhs.shape[1:]
    width = inverse_t.shape[2]
    blocks = 2 * lanes
    group = rhs_count // blocks
    half = rhs_count // 2
    levels_of = [trailing_ones(node) for node in range(members)]
    nodes_at = [[node for node in range(members) if levels_of[node] == s] for s in range(levels + 1)]
    leaves = nodes_at[0]
    inner = [node for node in range(members) if levels_of[node] > 0]

    def place():
        at = lax.axis_index("col")
        core, lane = at % 2, at // 2 % lanes
        return at // blocks, lane, core, core * lanes + lane

    def height():
        at, rank = lax.axis_index("lvl"), 0
        for s in range(1, levels + 1):
            rank = rank + ((at + 1) % 2**s == 0).astype(jnp.int32)
        return rank

    def permute(x, moves):
        pairs = []
        for plane in range(members):
            target, offset = moves.get(plane, (plane, 1))
            pairs += [(plane * cols + c, target * cols + (c ^ offset)) for c in range(cols)]
        return lax.ppermute(x, ("lvl", "col"), pairs)

    def across(x, offset, planes):
        return permute(x, {plane: (plane, offset) for plane in planes})

    def along(x, links, offset=0):
        moves = {}
        for a, b in links:
            moves[a], moves[b] = (b, offset), (a, offset)
        return permute(x, moves)

    def from_parent(left, right, section):
        return jnp.where(lax.axis_index("lvl") // 2**section % 2 == 0, left, right)

    def down(links):
        return [(b, a) for a, b in links]

    def after(x, *earlier):
        return lax.optimization_barrier((x, *earlier))[0]

    def over_chips(mine):
        return [mine] + [across(mine, 2 * chip, leaves) for chip in range(1, chips)]

    def over_rows(mine, planes):
        return [mine] + [across(mine, offset, planes) for offset in range(2 * lanes, cols, 2 * lanes)]

    def chip_total(refs):
        parts = []
        for i in range(lanes):
            total = refs[0][i * group : (i + 1) * group, :].astype(F32)
            for chip in range(1, chips):
                k = i ^ (chip % lanes)
                total = total + refs[chip][k * group : (k + 1) * group, :].astype(F32)
            parts.append(total)
        return jnp.concatenate(parts, axis=0)

    def row_total(refs):
        total = refs[0][...].astype(F32)
        for ref in refs[1:]:
            total = total + ref[...].astype(F32)
        return total

    def total_of(parts):
        total = parts[0]
        for part in parts[1:]:
            total = total + part
        return total

    def span(b):
        return slice(b * row_count, (b + 1) * row_count)

    def groups(b):
        return pl.ds(pl.multiple_of((b ^ place()[3]) * group, group), group)

    inverse_own, rhs_own = inverse_t[0], rhs[0]
    chip_rows = len(range(0, cols, 2 * lanes))

    def leaf_first(ins, outs, turned, ordered):
        turned[...] = ins[0][...].T
        for b in range(blocks):
            ordered[b * group : (b + 1) * group, :] = turned[groups(b), :]
        terms = ordered[...].astype(BF16)
        outs[0][...] = mm(terms[:half], ins[1][...]).astype(BF16)
        outs[1][...] = mm(terms[half:], ins[1][...]).astype(BF16)

    keep, give = call(
        leaf_first,
        [((half, width), BF16)] * 2,
        [rhs_own, inverse_own],
        [pltpu.VMEM((rhs_count, row_count), F32)] * 2,
    )
    got = across(give, 1, leaves)

    tiles = pattern.shape[-1]
    tile = width // tiles

    def build(ins, outs):
        pattern_ref, _, rhs_ref, inv_ref, panel_ref = ins
        first_row = lax.axis_index("col") * row_count
        row_ids = lax.broadcasted_iota(jnp.int32, (row_count, tiles), 0) + first_row
        row_tile = lax.broadcasted_iota(jnp.int32, (row_count, tiles), 1)
        row_pick = ((row_ids >= row_tile * tile) & (row_ids < (row_tile + 1) * tile)).astype(F32).astype(BF16)
        col_ids = lax.broadcasted_iota(jnp.int32, (tiles, width), 1)
        col_tile = lax.broadcasted_iota(jnp.int32, (tiles, width), 0)
        col_pick = ((col_ids >= col_tile * tile) & (col_ids < (col_tile + 1) * tile)).astype(F32).astype(BF16)
        masks = []
        for k in range(levels):
            kept = mm(row_pick, pattern_ref[0, k].astype(F32).astype(BF16)).astype(BF16)
            masks.append(mm(kept, col_pick).astype(BF16))
        high = rhs_ref[...].astype(BF16)
        low = (rhs_ref[...] - high.astype(F32)).astype(BF16)
        outs[0][:, levels * width : levels * width + rhs_count] = high
        outs[0][:, levels * width + rhs_count :] = low
        for k in range(levels):
            block = panel_ref[0, k] * masks[k]
            if k == last:
                block = jnp.where(height() == 0, block, inv_ref[...])
            outs[0][:, k * width : (k + 1) * width] = block
            if k < last:
                outs[1][:, k * width : (k + 1) * width] = jnp.where(height() == 1, block, inv_ref[...])

    full = levels * width + 2 * rhs_count
    rows_own, rows_sent = call(
        build,
        [((row_count, full), BF16), ((row_count, last * width), BF16)],
        [pattern, give, rhs_own, inverse_own, panel],
    )
    rows_own, rows_sent = after((rows_own, rows_sent), got)
    rows_far = across(rows_own, 1, range(members))
    rows_lanes = [across(rows_sent, 2 * i, inner) for i in range(1, lanes)]
    chip_part = (keep.astype(F32) + got.astype(F32)).astype(BF16)
    terms = over_chips(chip_part)

    def factor_of(ref, k):
        return ref[:, k * width : (k + 1) * width]

    def inverse_of(ref):
        return factor_of(ref, last) if ref.shape[1] == full else ref[:, :width]

    rounds = leaf_rounds(members)

    def leaf_push(ins, outs):
        solved = chip_total(ins[:chips]).astype(BF16)
        outs[0][...] = solved
        for n, sends in enumerate(rounds):
            slot = total_of([jnp.where(lax.axis_index("lvl") == leaf, k, 0) for leaf, k, _ in sends])
            columns = pl.ds(pl.multiple_of(slot * width, width), width)
            for j in range(2):
                outs[1 + n][:, span(j)] = mmt(solved, ins[chips + j][:, columns]).astype(BF16)

    vector = ((blocks, group, row_count), F32)
    term = ((group, width), BF16)
    leaf_half, *pushed = call(
        leaf_push,
        [((half, width), BF16)] + [((half, 2 * row_count), BF16)] * len(rounds),
        [*terms, rows_own, rows_far],
    )
    early = [along(sent, [(a, b) for a, _, b in sends]) for sent, sends in zip(pushed, rounds)]

    def heard(n, part):
        targets = [b for _, _, b in rounds[n]]
        if len(targets) == len(inner):
            return part
        here = total_of([(lax.axis_index("lvl") == b).astype(jnp.int32) for b in targets]) > 0
        return jnp.where(here, part, 0.0)

    def inner_first(ins, outs):
        came, pair = ins[:-2], ins[-2:]
        own = lax.broadcasted_iota(jnp.int32, (half, rhs_count), 0)
        at = lax.broadcasted_iota(jnp.int32, (half, rhs_count), 1)
        pick = jnp.zeros((half, rhs_count), F32)
        for i in range(lanes):
            mine = (own >= i * group) & (own < (i + 1) * group)
            spot = own - i * group + (i ^ place()[3]) * group
            pick = jnp.where(mine & (at == spot), 1.0, pick)
        pick = pick.astype(BF16)
        parts = []
        for j in range(2):
            rhs_pair = pair[j][:, levels * width :]
            side = mmt(pick, rhs_pair[:, :rhs_count]) + mmt(pick, rhs_pair[:, rhs_count:])
            less = total_of([heard(n, ref[:, span(j)].astype(F32)) for n, ref in enumerate(came)])
            parts.append(mm((side - less).astype(BF16), inverse_of(pair[j])))
        product = total_of(parts).astype(BF16)
        for i in range(lanes):
            outs[i][...] = product[i * group : (i + 1) * group]

    def by_lane(ins, outs):
        total = row_total(ins).astype(BF16)
        outs[0][...] = total

    leaf_lanes = [across(after(rows_own, leaf_half), 2 * i, leaves) for i in range(1, lanes)]
    first_rows = [rows_own, rows_far]
    for near in rows_lanes:
        first_rows += [near, across(after(near, *early), 1, inner)]
    early[0] = after(early[0], *rows_lanes)
    own_term, *others = call(inner_first, [term] * lanes, [*early, rows_own, rows_far])
    leaf_rows_of = [rows_own, rows_far]
    own_term = call(by_lane, term, [own_term] + [across(others[i - 1], 2 * i, inner) for i in range(1, lanes)])
    first_terms = over_rows(own_term, inner)
    first_terms[0] = after(first_terms[0], *leaf_lanes)
    leaf_far = across(after(leaf_half, own_term), 1, leaves)

    def spread(matrix, planes, wait, wait_far):
        parts = [rows_own, rows_far]
        for i in range(1, lanes):
            near = across(after(matrix, wait), 2 * i, planes)
            parts += [near, across(after(near, wait_far), 1, planes)]
        return parts

    samples = {}
    arrived = []
    for section in range(1, levels + 1):
        remain = levels - section
        nodes = nodes_at[section]
        terms = list(first_terms)
        if arrived:

            def inner_second(ins, outs):
                came, rows_of = ins[:-blocks], ins[-blocks:]
                parts = []
                for b in range(blocks):
                    less = total_of([ref[0, :, span(b)].astype(F32) for ref in came])
                    parts.append(mm(less.astype(BF16), inverse_of(rows_of[b])))
                outs[0][...] = (-total_of(parts)).astype(BF16)

            terms += over_rows(call(inner_second, term, [*arrived, *first_rows]), nodes)
        count = len(terms)
        if remain:

            def inner_push(ins, outs):
                solved = row_total(ins[:count])
                came, rows_of = ins[count:-blocks], ins[-blocks:]
                outs[0][...] = solved
                short = solved.astype(BF16)
                for k in range(remain):
                    for b in range(blocks):
                        product = mmt(short, factor_of(rows_of[b], k))
                        if came:
                            product = product + total_of([ref[k + 1, :, span(b)].astype(F32) for ref in came])
                        outs[1][k, :, span(b)] = product.astype(BF16)

            samples[section], sent = call(
                inner_push,
                [((group, width), F32), ((remain, group, blocks * row_count), BF16)],
                [*terms, *arrived, *(first_rows if section == 1 else higher_rows)],
            )
            arrived = [along(sent, links) for links in child_links(section + 1, members)]
            if section == 1:
                second_rows = spread(inverse_own, nodes_at[1], own_term, arrived[0])
                for near in leaf_lanes:
                    leaf_rows_of += [near, across(after(near, arrived[0]), 1, leaves)]
                arrived[0] = after(arrived[0], *second_rows[2::2])
                higher = [node for node in inner if 1 < levels_of[node] < levels]
                higher_rows = spread(rows_own[:, : last * width], higher, sent, sent) if higher else []

    def root_back(ins, outs):
        solved = row_total(ins[:-blocks])
        outs[0][...] = solved
        short = solved.astype(BF16)
        for b in range(blocks):
            answer = mmt(short, inverse_of(ins[b - blocks]))
            outs[1][b] = answer
            outs[2][0, :, span(b)] = answer.astype(BF16)

    samples[levels], answer, sent = call(
        root_back,
        [((group, width), F32), vector, ((1, group, blocks * row_count), BF16)],
        [*terms, *first_rows],
    )


    def split_rows(ins, outs):
        rank = height()
        solved = ins[0][...]
        for s in range(2, levels + 1):
            solved = jnp.where(rank == s, ins[s - 1][...], solved)
        high = solved.astype(BF16)
        stacked = jnp.concatenate([high, (solved - high.astype(F32)).astype(BF16)], axis=0)
        row, lane, core, _ = place()
        for b in range(blocks):
            start = (row * blocks + (b ^ (lane * 2 + core))) * row_count
            at = lax.broadcasted_iota(jnp.int32, (row_count, width), 0) + start
            pick = (lax.broadcasted_iota(jnp.int32, (row_count, width), 1) == at).astype(F32).astype(BF16)
            both = mmt(stacked, pick)
            outs[0][b] = both[:group] + both[group:]

    for section in range(levels - 1, 0, -1):
        remain = levels - section
        ancestry = [along(sent, down(links)) for links in child_links(section + 1, members)]
        ancestry = ancestry[0] if len(ancestry) == 1 else from_parent(*ancestry, section + 1)
        if section == 1:
            ancestry = after(ancestry, *second_rows)

        def adjoint_first(ins, outs):
            parts = []
            for b in range(blocks):
                for k in range(remain):
                    parts.append(mm(ins[0][k, :, span(b)], factor_of(ins[1 + b], k)))
            outs[0][...] = total_of(parts).astype(BF16)

        own_term = call(adjoint_first, term, [ancestry, *(first_rows if section == 1 else higher_rows)])
        terms = over_rows(own_term, nodes_at[section])
        if section == 1:
            order = [after(samples[s], own_term) for s in range(1, levels + 1)]
            sample_rows = call(split_rows, vector, order)

        def inner_back(ins, outs):
            came, ins = ins[:chip_rows], ins[chip_rows:]
            (solved, anc, higher), rows_of = ins[:3], ins[3 : 3 + blocks]
            back = (solved[...] - row_total(came)).astype(BF16)
            rank = height()
            outs[0][1:] = anc[...]
            for b in range(blocks):
                mine = mmt(back, inverse_of(rows_of[b]))
                outs[0][0, :, span(b)] = mine.astype(BF16)
                chosen = jnp.where(rank == section, mine, higher[b])
                if section == 1:
                    outs[1 + b][0] = ins[-1][b]
                    outs[1 + b][1] = chosen
                else:
                    outs[1][b] = chosen

        args = [*terms, samples[section], ancestry, answer, *(second_rows if section == 1 else first_rows)]
        outs = [((remain + 1, group, blocks * row_count), BF16)]
        if section == 1:
            args, outs = [*args, sample_rows], outs + [((2, group, row_count), F32)] * blocks
        else:
            outs = [*outs, vector]
        sent, *results = call(inner_back, outs, args)
        answer = results[0]

    ancestry = [along(sent, down(links)) for links in child_links(1, members)]

    def leaf_adjoint(ins, outs):
        came, rows_of = ins[:-blocks], ins[-blocks:]
        parts = []
        for b in range(blocks):
            for k in range(levels):
                parts.append(mm(from_parent(*[ref[k, :, span(b)] for ref in came], 1), factor_of(rows_of[b], k)))
        outs[0][...] = total_of(parts).astype(BF16)

    own_term = call(leaf_adjoint, term, [*ancestry, *leaf_rows_of])
    terms = over_rows(own_term, leaves)

    def in_order(near, far, whole):
        for b in range(blocks):
            source = near if b < lanes else far
            whole[groups(b), :] = source[b % lanes * group : (b % lanes + 1) * group, :]

    def leaf_rows(ins, outs, whole):
        in_order(ins[0], ins[1], whole)
        at = lax.broadcasted_iota(jnp.int32, (row_count, width), 0) + lax.axis_index("col") * row_count
        pick = (lax.broadcasted_iota(jnp.int32, (row_count, width), 1) == at).astype(F32).astype(BF16)
        outs[0][...] = mmt(pick, whole[...])

    whole_half = [pltpu.VMEM((rhs_count, width), BF16)]
    leaf_sample = call(leaf_rows, ((row_count, rhs_count), F32), [leaf_half, leaf_far], whole_half)

    parts = [results[0]] + [across(results[b], b, inner) for b in range(1, blocks)]

    def join_groups(ins, outs, whole):
        for n in range(2):
            for b in range(blocks):
                whole[groups(b % 2 * lanes + b // 2), :] = ins[b][n]
            outs[n][...] = whole[...].T

    shape = ((row_count, rhs_count), F32)
    inner_sample, inner_answer = call(
        join_groups, [shape] * 2, parts, [pltpu.VMEM((rhs_count, row_count), F32)]
    )

    def leaf_back(ins, outs):
        mine = ins[0][:group, :].astype(F32)
        outs[0][...] = (mine - row_total(ins[1:])).astype(BF16)

    terms[0] = after(terms[0], inner_sample, inner_answer, leaf_sample)
    back = call(leaf_back, term, [leaf_half, *terms])
    backs = [back] + [across(back, b, leaves) for b in range(1, blocks)]

    def leaf_last(ins, outs, whole):
        leaf_ref, inner_ref, answer_ref, inv_ref = ins[blocks:]
        for b in range(blocks):
            whole[groups(b % 2 * lanes + b // 2), :] = ins[b][...]
        is_leaf = height() == 0
        outs[0][...] = jnp.where(is_leaf, leaf_ref[...], inner_ref[...])
        outs[1][...] = jnp.where(is_leaf, mmt(inv_ref[...], whole[...]), answer_ref[...])

    sample, answer = call(
        leaf_last,
        [shape] * 2,
        [*backs, leaf_sample, inner_sample, inner_answer, inverse_own],
        whole_half,
    )
    return (sample[None], answer[None])


def solution(mesh):
    in_specs = (
        P("lvl", "col", None),
        P("lvl", None, "col", None),
        P("lvl", "col", None),
        P("lvl", None, None, None),
    )
    out_specs = (P("lvl", "col", None), P("lvl", "col", None))
    return jax.shard_map(
        on_device, mesh=mesh, in_specs=in_specs, out_specs=out_specs, check_vma=False
    )
```

```python
import jax
import jax.numpy as jnp
from jax import lax
from jax.experimental import pallas as pl
from jax.experimental.pallas import tpu as pltpu
from jax.sharding import PartitionSpec as P

F32 = jnp.float32
BF16 = jnp.bfloat16


def trailing_ones(node):
    ones = 0
    while node % 2 == 1:
        ones += 1
        node //= 2
    return ones


def child_links(section, members):
    reach = 2 ** (section - 1)
    parents = [node for node in range(members) if trailing_ones(node) == section]
    links = [[(node - reach, node) for node in parents], [(node + reach, node) for node in parents]]
    return [[(a, b) for a, b in side if a < members] for side in links if any(a < members for a, b in side)]


def leaf_rounds(members):
    rounds = []
    for leaf in range(0, members, 2):
        node, slot = leaf, 0
        while node != members - 1:
            reach = 2 ** trailing_ones(node)
            node += reach if node // (2 * reach) % 2 == 0 else -reach
            for sends in rounds:
                if all(leaf != a and node != b for a, _, b in sends):
                    break
            else:
                sends = []
                rounds.append(sends)
            sends.append((leaf, slot, node))
            slot += 1
    return rounds


def mm(a, b):
    return jnp.dot(a, b, preferred_element_type=F32)


def mmt(a, b):
    return lax.dot_general(a, b, (((1,), (1,)), ((), ())), preferred_element_type=F32)


def call(body, outs, args, scratch=()):
    single = isinstance(outs, tuple)
    shapes = [outs] if single else outs

    def kernel(*refs):
        middle = len(args) + len(shapes)
        body(refs[: len(args)], refs[len(args) : middle], *refs[middle:])

    moved = sum(a.size * a.dtype.itemsize for a in args)
    result = pl.pallas_call(
        kernel,
        out_shape=[jax.ShapeDtypeStruct(shape, dtype) for shape, dtype in shapes],
        in_specs=[pl.BlockSpec(memory_space=pltpu.VMEM) for _ in args],
        out_specs=[pl.BlockSpec(memory_space=pltpu.VMEM) for _ in shapes],
        scratch_shapes=list(scratch),
        compiler_params=pltpu.CompilerParams(vmem_limit_bytes=24 << 20),
        cost_estimate=pl.CostEstimate(flops=1 << 28, bytes_accessed=moved, transcendentals=0),
    )(*args)
    return result[0] if single else result


def on_device(rhs, panel, inverse_t, pattern):
    members = lax.axis_size("lvl")
    cols = lax.axis_size("col")
    levels = members.bit_length() - 1
    last = levels - 1
    chips = cols // 2
    lanes = 1 << ((chips.bit_length() - 1) // 2)
    row_count, rhs_count = rhs.shape[1:]
    width = inverse_t.shape[2]
    blocks = 2 * lanes
    group = rhs_count // blocks
    half = rhs_count // 2
    levels_of = [trailing_ones(node) for node in range(members)]
    nodes_at = [[node for node in range(members) if levels_of[node] == s] for s in range(levels + 1)]
    leaves = nodes_at[0]
    inner = [node for node in range(members) if levels_of[node] > 0]

    def place():
        at = lax.axis_index("col")
        core, lane = at % 2, at // 2 % lanes
        return at // blocks, lane, core, core * lanes + lane

    def height():
        at, rank = lax.axis_index("lvl"), 0
        for s in range(1, levels + 1):
            rank = rank + ((at + 1) % 2**s == 0).astype(jnp.int32)
        return rank

    def permute(x, moves):
        pairs = []
        for plane in range(members):
            target, offset = moves.get(plane, (plane, 1))
            pairs += [(plane * cols + c, target * cols + (c ^ offset)) for c in range(cols)]
        return lax.ppermute(x, ("lvl", "col"), pairs)

    def across(x, offset, planes):
        return permute(x, {plane: (plane, offset) for plane in planes})

    def along(x, links, offset=0):
        moves = {}
        for a, b in links:
            moves[a], moves[b] = (b, offset), (a, offset)
        return permute(x, moves)

    def from_parent(left, right, section):
        return jnp.where(lax.axis_index("lvl") // 2**section % 2 == 0, left, right)

    def down(links):
        return [(b, a) for a, b in links]

    def after(x, *earlier):
        return lax.optimization_barrier((x, *earlier))[0]

    def over_chips(mine):
        return [mine] + [across(mine, 2 * chip, leaves) for chip in range(1, chips)]

    def over_rows(mine, planes):
        return [mine] + [across(mine, offset, planes) for offset in range(2 * lanes, cols, 2 * lanes)]

    def chip_total(refs):
        parts = []
        for i in range(lanes):
            total = refs[0][i * group : (i + 1) * group, :].astype(F32)
            for chip in range(1, chips):
                k = i ^ (chip % lanes)
                total = total + refs[chip][k * group : (k + 1) * group, :].astype(F32)
            parts.append(total)
        return jnp.concatenate(parts, axis=0)

    def row_total(refs):
        total = refs[0][...].astype(F32)
        for ref in refs[1:]:
            total = total + ref[...].astype(F32)
        return total

    def total_of(parts):
        total = parts[0]
        for part in parts[1:]:
            total = total + part
        return total

    def span(b):
        return slice(b * row_count, (b + 1) * row_count)

    def groups(b):
        return pl.ds(pl.multiple_of((b ^ place()[3]) * group, group), group)

    inverse_own, rhs_own = inverse_t[0], rhs[0]
    chip_rows = len(range(0, cols, 2 * lanes))

    def leaf_first(ins, outs, turned, ordered):
        turned[...] = ins[0][...].T
        for b in range(blocks):
            ordered[b * group : (b + 1) * group, :] = turned[groups(b), :]
        terms = ordered[...].astype(BF16)
        outs[0][...] = mm(terms[:half], ins[1][...]).astype(BF16)
        outs[1][...] = mm(terms[half:], ins[1][...]).astype(BF16)

    keep, give = call(
        leaf_first,
        [((half, width), BF16)] * 2,
        [rhs_own, inverse_own],
        [pltpu.VMEM((rhs_count, row_count), F32)] * 2,
    )
    got = across(give, 1, leaves)

    tiles = pattern.shape[-1]
    tile = width // tiles

    def build(ins, outs):
        pattern_ref, _, rhs_ref, inv_ref, panel_ref = ins
        first_row = lax.axis_index("col") * row_count
        row_ids = lax.broadcasted_iota(jnp.int32, (row_count, tiles), 0) + first_row
        row_tile = lax.broadcasted_iota(jnp.int32, (row_count, tiles), 1)
        row_pick = ((row_ids >= row_tile * tile) & (row_ids < (row_tile + 1) * tile)).astype(F32).astype(BF16)
        col_ids = lax.broadcasted_iota(jnp.int32, (tiles, width), 1)
        col_tile = lax.broadcasted_iota(jnp.int32, (tiles, width), 0)
        col_pick = ((col_ids >= col_tile * tile) & (col_ids < (col_tile + 1) * tile)).astype(F32).astype(BF16)
        masks = []
        for k in range(levels):
            kept = mm(row_pick, pattern_ref[0, k].astype(F32).astype(BF16)).astype(BF16)
            masks.append(mm(kept, col_pick).astype(BF16))
        high = rhs_ref[...].astype(BF16)
        low = (rhs_ref[...] - high.astype(F32)).astype(BF16)
        outs[0][:, levels * width : levels * width + rhs_count] = high
        outs[0][:, levels * width + rhs_count :] = low
        for k in range(levels):
            block = panel_ref[0, k] * masks[k]
            if k == last:
                block = jnp.where(height() == 0, block, inv_ref[...])
            outs[0][:, k * width : (k + 1) * width] = block
            if k < last:
                outs[1][:, k * width : (k + 1) * width] = jnp.where(height() == 1, block, inv_ref[...])

    full = levels * width + 2 * rhs_count
    rows_own, rows_sent = call(
        build,
        [((row_count, full), BF16), ((row_count, last * width), BF16)],
        [pattern, give, rhs_own, inverse_own, panel],
    )
    rows_own, rows_sent = after((rows_own, rows_sent), got)
    rows_far = across(rows_own, 1, range(members))
    rows_lanes = [across(rows_sent, 2 * i, inner) for i in range(1, lanes)]
    chip_part = (keep.astype(F32) + got.astype(F32)).astype(BF16)
    terms = over_chips(chip_part)

    def factor_of(ref, k):
        return ref[:, k * width : (k + 1) * width]

    def inverse_of(ref):
        return factor_of(ref, last) if ref.shape[1] == full else ref[:, :width]

    rounds = leaf_rounds(members)

    def leaf_push(ins, outs):
        solved = chip_total(ins[:chips]).astype(BF16)
        outs[0][...] = solved
        for n, sends in enumerate(rounds):
            slot = total_of([jnp.where(lax.axis_index("lvl") == leaf, k, 0) for leaf, k, _ in sends])
            columns = pl.ds(pl.multiple_of(slot * width, width), width)
            for j in range(2):
                outs[1 + n][:, span(j)] = mmt(solved, ins[chips + j][:, columns]).astype(BF16)

    vector = ((blocks, group, row_count), F32)
    term = ((group, width), BF16)
    leaf_half, *pushed = call(
        leaf_push,
        [((half, width), BF16)] + [((half, 2 * row_count), BF16)] * len(rounds),
        [*terms, rows_own, rows_far],
    )
    early = [along(sent, [(a, b) for a, _, b in sends]) for sent, sends in zip(pushed, rounds)]

    def heard(n, part):
        targets = [b for _, _, b in rounds[n]]
        if len(targets) == len(inner):
            return part
        here = total_of([(lax.axis_index("lvl") == b).astype(jnp.int32) for b in targets]) > 0
        return jnp.where(here, part, 0.0)

    def inner_first(ins, outs):
        came, pair = ins[:-2], ins[-2:]
        own = lax.broadcasted_iota(jnp.int32, (half, rhs_count), 0)
        at = lax.broadcasted_iota(jnp.int32, (half, rhs_count), 1)
        pick = jnp.zeros((half, rhs_count), F32)
        for i in range(lanes):
            mine = (own >= i * group) & (own < (i + 1) * group)
            spot = own - i * group + (i ^ place()[3]) * group
            pick = jnp.where(mine & (at == spot), 1.0, pick)
        pick = pick.astype(BF16)
        parts = []
        for j in range(2):
            rhs_pair = pair[j][:, levels * width :]
            side = mmt(pick, rhs_pair[:, :rhs_count]) + mmt(pick, rhs_pair[:, rhs_count:])
            less = total_of([heard(n, ref[:, span(j)].astype(F32)) for n, ref in enumerate(came)])
            parts.append(mm((side - less).astype(BF16), inverse_of(pair[j])))
        product = total_of(parts).astype(BF16)
        for i in range(lanes):
            outs[i][...] = product[i * group : (i + 1) * group]

    def by_lane(ins, outs):
        total = row_total(ins).astype(BF16)
        outs[0][...] = total

    leaf_lanes = [across(after(rows_own, leaf_half), 2 * i, leaves) for i in range(1, lanes)]
    own_term, *others = call(inner_first, [term] * lanes, [*early, rows_own, rows_far])
    first_rows = [rows_own, rows_far]
    for near in rows_lanes:
        first_rows += [near, across(after(near, own_term), 1, inner)]
    leaf_rows_of = [rows_own, rows_far]
    own_term = call(by_lane, term, [own_term] + [across(others[i - 1], 2 * i, inner) for i in range(1, lanes)])
    first_terms = over_rows(own_term, inner)
    leaf_far = across(after(leaf_half, own_term), 1, leaves)

    def spread(matrix, planes, wait, wait_far):
        parts = [rows_own, rows_far]
        for i in range(1, lanes):
            near = across(after(matrix, wait), 2 * i, planes)
            parts += [near, across(after(near, wait_far), 1, planes)]
        return parts

    samples = {}
    arrived = []
    for section in range(1, levels + 1):
        remain = levels - section
        nodes = nodes_at[section]
        terms = list(first_terms)
        if arrived:

            def inner_second(ins, outs):
                came, rows_of = ins[:-blocks], ins[-blocks:]
                parts = []
                for b in range(blocks):
                    less = total_of([ref[0, :, span(b)].astype(F32) for ref in came])
                    parts.append(mm(less.astype(BF16), inverse_of(rows_of[b])))
                outs[0][...] = (-total_of(parts)).astype(BF16)

            terms += over_rows(call(inner_second, term, [*arrived, *first_rows]), nodes)
        count = len(terms)
        if remain:

            def inner_push(ins, outs):
                solved = row_total(ins[:count])
                came, rows_of = ins[count:-blocks], ins[-blocks:]
                outs[0][...] = solved
                short = solved.astype(BF16)
                for k in range(remain):
                    for b in range(blocks):
                        product = mmt(short, factor_of(rows_of[b], k))
                        if came:
                            product = product + total_of([ref[k + 1, :, span(b)].astype(F32) for ref in came])
                        outs[1][k, :, span(b)] = product.astype(BF16)

            samples[section], sent = call(
                inner_push,
                [((group, width), F32), ((remain, group, blocks * row_count), BF16)],
                [*terms, *arrived, *(first_rows if section == 1 else higher_rows)],
            )
            arrived = [along(sent, links) for links in child_links(section + 1, members)]
            if section == 1:
                second_rows = spread(inverse_own, nodes_at[1], own_term, arrived[0])
                for near in leaf_lanes:
                    leaf_rows_of += [near, across(after(near, arrived[0]), 1, leaves)]
                arrived[0] = after(arrived[0], *second_rows[2::2], *leaf_lanes)
                higher = [node for node in inner if 1 < levels_of[node] < levels]
                higher_rows = spread(rows_own[:, : last * width], higher, sent, sent) if higher else []

    def root_back(ins, outs):
        solved = row_total(ins[:-blocks])
        outs[0][...] = solved
        short = solved.astype(BF16)
        for b in range(blocks):
            answer = mmt(short, inverse_of(ins[b - blocks]))
            outs[1][b] = answer
            outs[2][0, :, span(b)] = answer.astype(BF16)

    samples[levels], answer, sent = call(
        root_back,
        [((group, width), F32), vector, ((1, group, blocks * row_count), BF16)],
        [*terms, *first_rows],
    )


    def split_rows(ins, outs):
        rank = height()
        solved = ins[0][...]
        for s in range(2, levels + 1):
            solved = jnp.where(rank == s, ins[s - 1][...], solved)
        high = solved.astype(BF16)
        stacked = jnp.concatenate([high, (solved - high.astype(F32)).astype(BF16)], axis=0)
        row, lane, core, _ = place()
        for b in range(blocks):
            start = (row * blocks + (b ^ (lane * 2 + core))) * row_count
            at = lax.broadcasted_iota(jnp.int32, (row_count, width), 0) + start
            pick = (lax.broadcasted_iota(jnp.int32, (row_count, width), 1) == at).astype(F32).astype(BF16)
            both = mmt(stacked, pick)
            outs[0][b] = both[:group] + both[group:]

    for section in range(levels - 1, 0, -1):
        remain = levels - section
        ancestry = [along(sent, down(links)) for links in child_links(section + 1, members)]
        ancestry = ancestry[0] if len(ancestry) == 1 else from_parent(*ancestry, section + 1)
        if section == 1:
            ancestry = after(ancestry, *second_rows)

        def adjoint_first(ins, outs):
            parts = []
            for b in range(blocks):
                for k in range(remain):
                    parts.append(mm(ins[0][k, :, span(b)], factor_of(ins[1 + b], k)))
            outs[0][...] = total_of(parts).astype(BF16)

        own_term = call(adjoint_first, term, [ancestry, *(first_rows if section == 1 else higher_rows)])
        terms = over_rows(own_term, nodes_at[section])
        if section == 1:
            order = [after(samples[s], own_term) for s in range(1, levels + 1)]
            sample_rows = call(split_rows, vector, order)

        def inner_back(ins, outs):
            came, ins = ins[:chip_rows], ins[chip_rows:]
            (solved, anc, higher), rows_of = ins[:3], ins[3 : 3 + blocks]
            back = (solved[...] - row_total(came)).astype(BF16)
            rank = height()
            outs[0][1:] = anc[...]
            for b in range(blocks):
                mine = mmt(back, inverse_of(rows_of[b]))
                outs[0][0, :, span(b)] = mine.astype(BF16)
                chosen = jnp.where(rank == section, mine, higher[b])
                if section == 1:
                    outs[1 + b][0] = ins[-1][b]
                    outs[1 + b][1] = chosen
                else:
                    outs[1][b] = chosen

        args = [*terms, samples[section], ancestry, answer, *(second_rows if section == 1 else first_rows)]
        outs = [((remain + 1, group, blocks * row_count), BF16)]
        if section == 1:
            args, outs = [*args, sample_rows], outs + [((2, group, row_count), F32)] * blocks
        else:
            outs = [*outs, vector]
        sent, *results = call(inner_back, outs, args)
        answer = results[0]

    ancestry = [along(sent, down(links)) for links in child_links(1, members)]

    def leaf_adjoint(ins, outs):
        came, rows_of = ins[:-blocks], ins[-blocks:]
        parts = []
        for b in range(blocks):
            for k in range(levels):
                parts.append(mm(from_parent(*[ref[k, :, span(b)] for ref in came], 1), factor_of(rows_of[b], k)))
        outs[0][...] = total_of(parts).astype(BF16)

    own_term = call(leaf_adjoint, term, [*ancestry, *leaf_rows_of])
    terms = over_rows(own_term, leaves)

    def in_order(near, far, whole):
        for b in range(blocks):
            source = near if b < lanes else far
            whole[groups(b), :] = source[b % lanes * group : (b % lanes + 1) * group, :]

    def leaf_rows(ins, outs, whole):
        in_order(ins[0], ins[1], whole)
        at = lax.broadcasted_iota(jnp.int32, (row_count, width), 0) + lax.axis_index("col") * row_count
        pick = (lax.broadcasted_iota(jnp.int32, (row_count, width), 1) == at).astype(F32).astype(BF16)
        outs[0][...] = mmt(pick, whole[...])

    whole_half = [pltpu.VMEM((rhs_count, width), BF16)]
    leaf_sample = call(leaf_rows, ((row_count, rhs_count), F32), [leaf_half, leaf_far], whole_half)

    parts = [results[0]] + [across(results[b], b, inner) for b in range(1, blocks)]

    def join_groups(ins, outs, whole):
        for n in range(2):
            for b in range(blocks):
                whole[groups(b % 2 * lanes + b // 2), :] = ins[b][n]
            outs[n][...] = whole[...].T

    shape = ((row_count, rhs_count), F32)
    inner_sample, inner_answer = call(
        join_groups, [shape] * 2, parts, [pltpu.VMEM((rhs_count, row_count), F32)]
    )

    def leaf_back(ins, outs):
        mine = ins[0][:group, :].astype(F32)
        outs[0][...] = (mine - row_total(ins[1:])).astype(BF16)

    terms[0] = after(terms[0], inner_sample, inner_answer, leaf_sample)
    back = call(leaf_back, term, [leaf_half, *terms])
    near = [back] + [across(back, 2 * i, leaves) for i in range(1, lanes)]
    near = jnp.concatenate(near, axis=0)
    far = across(near, 1, leaves)

    def leaf_last(ins, outs, whole):
        near_ref, far_ref, leaf_ref, inner_ref, answer_ref, inv_ref = ins
        in_order(near_ref, far_ref, whole)
        is_leaf = height() == 0
        outs[0][...] = jnp.where(is_leaf, leaf_ref[...], inner_ref[...])
        outs[1][...] = jnp.where(is_leaf, mmt(inv_ref[...], whole[...]), answer_ref[...])

    sample, answer = call(
        leaf_last,
        [shape] * 2,
        [near, far, leaf_sample, inner_sample, inner_answer, inverse_own],
        whole_half,
    )
    return (sample[None], answer[None])


def solution(mesh):
    in_specs = (
        P("lvl", "col", None),
        P("lvl", None, "col", None),
        P("lvl", "col", None),
        P("lvl", None, None, None),
    )
    out_specs = (P("lvl", "col", None), P("lvl", "col", None))
    return jax.shard_map(
        on_device, mesh=mesh, in_specs=in_specs, out_specs=out_specs, check_vma=False
    )
```

```python
import jax
import jax.numpy as jnp
from jax import lax
from jax.experimental import pallas as pl
from jax.experimental.pallas import tpu as pltpu
from jax.sharding import PartitionSpec as P

F32 = jnp.float32
BF16 = jnp.bfloat16


def trailing_ones(node):
    ones = 0
    while node % 2 == 1:
        ones += 1
        node //= 2
    return ones


def child_links(section, members):
    reach = 2 ** (section - 1)
    parents = [node for node in range(members) if trailing_ones(node) == section]
    links = [[(node - reach, node) for node in parents], [(node + reach, node) for node in parents]]
    return [[(a, b) for a, b in side if a < members] for side in links if any(a < members for a, b in side)]


def leaf_rounds(members):
    rounds = []
    for leaf in range(0, members, 2):
        node, slot = leaf, 0
        while node != members - 1:
            reach = 2 ** trailing_ones(node)
            node += reach if node // (2 * reach) % 2 == 0 else -reach
            for sends in rounds:
                if all(leaf != a and node != b for a, _, b in sends):
                    break
            else:
                sends = []
                rounds.append(sends)
            sends.append((leaf, slot, node))
            slot += 1
    return rounds


def mm(a, b):
    return jnp.dot(a, b, preferred_element_type=F32)


def mmt(a, b):
    return lax.dot_general(a, b, (((1,), (1,)), ((), ())), preferred_element_type=F32)


def call(body, outs, args, scratch=()):
    single = isinstance(outs, tuple)
    shapes = [outs] if single else outs

    def kernel(*refs):
        middle = len(args) + len(shapes)
        body(refs[: len(args)], refs[len(args) : middle], *refs[middle:])

    moved = sum(a.size * a.dtype.itemsize for a in args)
    result = pl.pallas_call(
        kernel,
        out_shape=[jax.ShapeDtypeStruct(shape, dtype) for shape, dtype in shapes],
        in_specs=[pl.BlockSpec(memory_space=pltpu.VMEM) for _ in args],
        out_specs=[pl.BlockSpec(memory_space=pltpu.VMEM) for _ in shapes],
        scratch_shapes=list(scratch),
        compiler_params=pltpu.CompilerParams(vmem_limit_bytes=24 << 20),
        cost_estimate=pl.CostEstimate(flops=1 << 28, bytes_accessed=moved, transcendentals=0),
    )(*args)
    return result[0] if single else result


def on_device(rhs, panel, inverse_t, pattern):
    members = lax.axis_size("lvl")
    cols = lax.axis_size("col")
    levels = members.bit_length() - 1
    last = levels - 1
    chips = cols // 2
    lanes = 1 << ((chips.bit_length() - 1) // 2)
    row_count, rhs_count = rhs.shape[1:]
    width = inverse_t.shape[2]
    blocks = 2 * lanes
    group = rhs_count // blocks
    half = rhs_count // 2
    levels_of = [trailing_ones(node) for node in range(members)]
    nodes_at = [[node for node in range(members) if levels_of[node] == s] for s in range(levels + 1)]
    leaves = nodes_at[0]
    inner = [node for node in range(members) if levels_of[node] > 0]

    def place():
        at = lax.axis_index("col")
        core, lane = at % 2, at // 2 % lanes
        return at // blocks, lane, core, core * lanes + lane

    def height():
        at, rank = lax.axis_index("lvl"), 0
        for s in range(1, levels + 1):
            rank = rank + ((at + 1) % 2**s == 0).astype(jnp.int32)
        return rank

    def permute(x, moves):
        pairs = []
        for plane in range(members):
            target, offset = moves.get(plane, (plane, 1))
            pairs += [(plane * cols + c, target * cols + (c ^ offset)) for c in range(cols)]
        return lax.ppermute(x, ("lvl", "col"), pairs)

    def across(x, offset, planes):
        return permute(x, {plane: (plane, offset) for plane in planes})

    def along(x, links, offset=0):
        moves = {}
        for a, b in links:
            moves[a], moves[b] = (b, offset), (a, offset)
        return permute(x, moves)

    def from_parent(left, right, section):
        return jnp.where(lax.axis_index("lvl") // 2**section % 2 == 0, left, right)

    def down(links):
        return [(b, a) for a, b in links]

    def after(x, *earlier):
        return lax.optimization_barrier((x, *earlier))[0]

    def over_chips(mine):
        return [mine] + [across(mine, 2 * chip, leaves) for chip in range(1, chips)]

    def over_rows(mine, planes):
        return [mine] + [across(mine, offset, planes) for offset in range(2 * lanes, cols, 2 * lanes)]

    def chip_total(refs):
        parts = []
        for i in range(lanes):
            total = refs[0][i * group : (i + 1) * group, :].astype(F32)
            for chip in range(1, chips):
                k = i ^ (chip % lanes)
                total = total + refs[chip][k * group : (k + 1) * group, :].astype(F32)
            parts.append(total)
        return jnp.concatenate(parts, axis=0)

    def row_total(refs):
        total = refs[0][...].astype(F32)
        for ref in refs[1:]:
            total = total + ref[...].astype(F32)
        return total

    def total_of(parts):
        total = parts[0]
        for part in parts[1:]:
            total = total + part
        return total

    def span(b):
        return slice(b * row_count, (b + 1) * row_count)

    def groups(b):
        return pl.ds(pl.multiple_of((b ^ place()[3]) * group, group), group)

    inverse_own, rhs_own = inverse_t[0], rhs[0]
    chip_rows = len(range(0, cols, 2 * lanes))

    def leaf_first(ins, outs, turned, ordered):
        turned[...] = ins[0][...].T
        for b in range(blocks):
            ordered[b * group : (b + 1) * group, :] = turned[groups(b), :]
        terms = ordered[...].astype(BF16)
        outs[0][...] = mm(terms[:half], ins[1][...]).astype(BF16)
        outs[1][...] = mm(terms[half:], ins[1][...]).astype(BF16)

    keep, give = call(
        leaf_first,
        [((half, width), BF16)] * 2,
        [rhs_own, inverse_own],
        [pltpu.VMEM((rhs_count, row_count), F32)] * 2,
    )
    got = across(give, 1, leaves)

    tiles = pattern.shape[-1]
    tile = width // tiles

    def build(ins, outs):
        pattern_ref, _, rhs_ref, inv_ref, panel_ref = ins
        first_row = lax.axis_index("col") * row_count
        row_ids = lax.broadcasted_iota(jnp.int32, (row_count, tiles), 0) + first_row
        row_tile = lax.broadcasted_iota(jnp.int32, (row_count, tiles), 1)
        row_pick = ((row_ids >= row_tile * tile) & (row_ids < (row_tile + 1) * tile)).astype(F32).astype(BF16)
        col_ids = lax.broadcasted_iota(jnp.int32, (tiles, width), 1)
        col_tile = lax.broadcasted_iota(jnp.int32, (tiles, width), 0)
        col_pick = ((col_ids >= col_tile * tile) & (col_ids < (col_tile + 1) * tile)).astype(F32).astype(BF16)
        masks = []
        for k in range(levels):
            kept = mm(row_pick, pattern_ref[0, k].astype(F32).astype(BF16)).astype(BF16)
            masks.append(mm(kept, col_pick).astype(BF16))
        high = rhs_ref[...].astype(BF16)
        low = (rhs_ref[...] - high.astype(F32)).astype(BF16)
        outs[0][:, levels * width : levels * width + rhs_count] = high
        outs[0][:, levels * width + rhs_count :] = low
        for k in range(levels):
            block = panel_ref[0, k] * masks[k]
            if k == last:
                block = jnp.where(height() == 0, block, inv_ref[...])
            outs[0][:, k * width : (k + 1) * width] = block
            if k < last:
                outs[1][:, k * width : (k + 1) * width] = jnp.where(height() == 1, block, inv_ref[...])

    full = levels * width + 2 * rhs_count
    rows_own, rows_sent = call(
        build,
        [((row_count, full), BF16), ((row_count, last * width), BF16)],
        [pattern, give, rhs_own, inverse_own, panel],
    )
    rows_own, rows_sent = after((rows_own, rows_sent), got)
    rows_far = across(rows_own, 1, range(members))
    rows_lanes = [across(rows_sent, 2 * i, inner) for i in range(1, lanes)]
    chip_part = (keep.astype(F32) + got.astype(F32)).astype(BF16)
    terms = over_chips(chip_part)

    def factor_of(ref, k):
        return ref[:, k * width : (k + 1) * width]

    def inverse_of(ref):
        return factor_of(ref, last) if ref.shape[1] == full else ref[:, :width]

    rounds = leaf_rounds(members)

    def leaf_push(ins, outs):
        solved = chip_total(ins[:chips]).astype(BF16)
        outs[0][...] = solved
        for n, sends in enumerate(rounds):
            slot = total_of([jnp.where(lax.axis_index("lvl") == leaf, k, 0) for leaf, k, _ in sends])
            columns = pl.ds(pl.multiple_of(slot * width, width), width)
            for j in range(2):
                outs[1 + n][:, span(j)] = mmt(solved, ins[chips + j][:, columns]).astype(BF16)

    vector = ((blocks, group, row_count), F32)
    term = ((group, width), BF16)
    leaf_half, *pushed = call(
        leaf_push,
        [((half, width), BF16)] + [((half, 2 * row_count), BF16)] * len(rounds),
        [*terms, rows_own, rows_far],
    )
    early = [along(sent, [(a, b) for a, _, b in sends]) for sent, sends in zip(pushed, rounds)]

    def heard(n, part):
        targets = [b for _, _, b in rounds[n]]
        if len(targets) == len(inner):
            return part
        here = total_of([(lax.axis_index("lvl") == b).astype(jnp.int32) for b in targets]) > 0
        return jnp.where(here, part, 0.0)

    def inner_first(ins, outs):
        came, pair = ins[:-2], ins[-2:]
        own = lax.broadcasted_iota(jnp.int32, (half, rhs_count), 0)
        at = lax.broadcasted_iota(jnp.int32, (half, rhs_count), 1)
        pick = jnp.zeros((half, rhs_count), F32)
        for i in range(lanes):
            mine = (own >= i * group) & (own < (i + 1) * group)
            spot = own - i * group + (i ^ place()[3]) * group
            pick = jnp.where(mine & (at == spot), 1.0, pick)
        pick = pick.astype(BF16)
        parts = []
        for j in range(2):
            rhs_pair = pair[j][:, levels * width :]
            side = mmt(pick, rhs_pair[:, :rhs_count]) + mmt(pick, rhs_pair[:, rhs_count:])
            less = total_of([heard(n, ref[:, span(j)].astype(F32)) for n, ref in enumerate(came)])
            parts.append(mm((side - less).astype(BF16), inverse_of(pair[j])))
        product = total_of(parts).astype(BF16)
        for i in range(lanes):
            outs[i][...] = product[i * group : (i + 1) * group]

    leaf_lanes = [across(after(rows_own, leaf_half), 2 * i, leaves) for i in range(1, lanes)]
    own_term, *others = call(inner_first, [term] * lanes, [*early, rows_own, rows_far])
    first_rows = [rows_own, rows_far]
    for near in rows_lanes:
        first_rows += [near, across(after(near, own_term), 1, inner)]
    leaf_rows_of = [rows_own, rows_far]
    by_lane = [own_term, *others]
    first_terms = [own_term] + [across(by_lane[chip % lanes], 2 * chip, inner) for chip in range(1, chips)]
    leaf_far = across(after(leaf_half, own_term), 1, leaves)

    def spread(matrix, planes, wait, wait_far):
        parts = [rows_own, rows_far]
        for i in range(1, lanes):
            near = across(after(matrix, wait), 2 * i, planes)
            parts += [near, across(after(near, wait_far), 1, planes)]
        return parts

    samples = {}
    arrived = []
    for section in range(1, levels + 1):
        remain = levels - section
        nodes = nodes_at[section]
        terms = list(first_terms)
        if arrived:

            def inner_second(ins, outs):
                came, rows_of = ins[:-blocks], ins[-blocks:]
                parts = []
                for b in range(blocks):
                    less = total_of([ref[0, :, span(b)].astype(F32) for ref in came])
                    parts.append(mm(less.astype(BF16), inverse_of(rows_of[b])))
                outs[0][...] = (-total_of(parts)).astype(BF16)

            terms += over_rows(call(inner_second, term, [*arrived, *first_rows]), nodes)
        count = len(terms)
        if remain:

            def inner_push(ins, outs):
                solved = row_total(ins[:count])
                came, rows_of = ins[count:-blocks], ins[-blocks:]
                outs[0][...] = solved
                short = solved.astype(BF16)
                for k in range(remain):
                    for b in range(blocks):
                        product = mmt(short, factor_of(rows_of[b], k))
                        if came:
                            product = product + total_of([ref[k + 1, :, span(b)].astype(F32) for ref in came])
                        outs[1][k, :, span(b)] = product.astype(BF16)

            samples[section], sent = call(
                inner_push,
                [((group, width), F32), ((remain, group, blocks * row_count), BF16)],
                [*terms, *arrived, *(first_rows if section == 1 else higher_rows)],
            )
            arrived = [along(sent, links) for links in child_links(section + 1, members)]
            if section == 1:
                second_lanes = [
                    across(after(inverse_own, first_terms[-1]), 2 * i, nodes_at[1]) for i in range(1, lanes)
                ]
                for near in leaf_lanes:
                    leaf_rows_of += [near, across(after(near, arrived[0]), 1, leaves)]
                arrived[0] = after(arrived[0], *leaf_lanes)
                higher = [node for node in inner if 1 < levels_of[node] < levels]
                higher_rows = spread(rows_own[:, : last * width], higher, sent, sent) if higher else []

    def root_back(ins, outs):
        solved = row_total(ins[:-blocks])
        outs[0][...] = solved
        short = solved.astype(BF16)
        for b in range(blocks):
            answer = mmt(short, inverse_of(ins[b - blocks]))
            outs[1][b] = answer
            outs[2][0, :, span(b)] = answer.astype(BF16)

    terms[0] = after(terms[0], *second_lanes)
    samples[levels], answer, sent = call(
        root_back,
        [((group, width), F32), vector, ((1, group, blocks * row_count), BF16)],
        [*terms, *first_rows],
    )


    second_rows = [rows_own, rows_far]
    for near in second_lanes:
        second_rows += [near, across(after(near, sent), 1, nodes_at[1])]

    def split_rows(ins, outs):
        rank = height()
        solved = ins[0][...]
        for s in range(2, levels + 1):
            solved = jnp.where(rank == s, ins[s - 1][...], solved)
        high = solved.astype(BF16)
        stacked = jnp.concatenate([high, (solved - high.astype(F32)).astype(BF16)], axis=0)
        row, lane, core, _ = place()
        for b in range(blocks):
            start = (row * blocks + (b ^ (lane * 2 + core))) * row_count
            at = lax.broadcasted_iota(jnp.int32, (row_count, width), 0) + start
            pick = (lax.broadcasted_iota(jnp.int32, (row_count, width), 1) == at).astype(F32).astype(BF16)
            both = mmt(stacked, pick)
            outs[0][b] = both[:group] + both[group:]

    for section in range(levels - 1, 0, -1):
        remain = levels - section
        ancestry = [along(sent, down(links)) for links in child_links(section + 1, members)]
        ancestry = ancestry[0] if len(ancestry) == 1 else from_parent(*ancestry, section + 1)

        def adjoint_first(ins, outs):
            parts = []
            for b in range(blocks):
                for k in range(remain):
                    parts.append(mm(ins[0][k, :, span(b)], factor_of(ins[1 + b], k)))
            outs[0][...] = total_of(parts).astype(BF16)

        own_term = call(adjoint_first, term, [ancestry, *(first_rows if section == 1 else higher_rows)])
        terms = over_rows(own_term, nodes_at[section])
        if section == 1:
            order = [after(samples[s], own_term) for s in range(1, levels + 1)]
            sample_rows = call(split_rows, vector, order)

        def inner_back(ins, outs):
            came, ins = ins[:chip_rows], ins[chip_rows:]
            (solved, anc, higher), rows_of = ins[:3], ins[3 : 3 + blocks]
            back = (solved[...] - row_total(came)).astype(BF16)
            rank = height()
            outs[0][1:] = anc[...]
            for b in range(blocks):
                mine = mmt(back, inverse_of(rows_of[b]))
                outs[0][0, :, span(b)] = mine.astype(BF16)
                chosen = jnp.where(rank == section, mine, higher[b])
                if section == 1:
                    outs[1 + b][0] = ins[-1][b]
                    outs[1 + b][1] = chosen
                else:
                    outs[1][b] = chosen

        args = [*terms, samples[section], ancestry, answer, *(second_rows if section == 1 else first_rows)]
        outs = [((remain + 1, group, blocks * row_count), BF16)]
        if section == 1:
            args, outs = [*args, sample_rows], outs + [((2, group, row_count), F32)] * blocks
        else:
            outs = [*outs, vector]
        sent, *results = call(inner_back, outs, args)
        answer = results[0]

    ancestry = [along(sent, down(links)) for links in child_links(1, members)]

    def leaf_adjoint(ins, outs):
        came, rows_of = ins[:-blocks], ins[-blocks:]
        parts = []
        for b in range(blocks):
            for k in range(levels):
                parts.append(mm(from_parent(*[ref[k, :, span(b)] for ref in came], 1), factor_of(rows_of[b], k)))
        outs[0][...] = total_of(parts).astype(BF16)

    own_term = call(leaf_adjoint, term, [*ancestry, *leaf_rows_of])
    terms = over_rows(own_term, leaves)

    def in_order(near, far, whole):
        for b in range(blocks):
            source = near if b < lanes else far
            whole[groups(b), :] = source[b % lanes * group : (b % lanes + 1) * group, :]

    def leaf_rows(ins, outs, whole):
        in_order(ins[0], ins[1], whole)
        at = lax.broadcasted_iota(jnp.int32, (row_count, width), 0) + lax.axis_index("col") * row_count
        pick = (lax.broadcasted_iota(jnp.int32, (row_count, width), 1) == at).astype(F32).astype(BF16)
        outs[0][...] = mmt(pick, whole[...])

    whole_half = [pltpu.VMEM((rhs_count, width), BF16)]
    leaf_sample = call(leaf_rows, ((row_count, rhs_count), F32), [leaf_half, leaf_far], whole_half)

    parts = [results[0]] + [across(results[b], b, inner) for b in range(1, blocks)]

    def join_groups(ins, outs, whole):
        for n in range(2):
            for b in range(blocks):
                whole[groups(b % 2 * lanes + b // 2), :] = ins[b][n]
            outs[n][...] = whole[...].T

    shape = ((row_count, rhs_count), F32)
    inner_sample, inner_answer = call(
        join_groups, [shape] * 2, parts, [pltpu.VMEM((rhs_count, row_count), F32)]
    )

    def leaf_back(ins, outs):
        mine = ins[0][:group, :].astype(F32)
        outs[0][...] = (mine - row_total(ins[1:])).astype(BF16)

    terms[0] = after(terms[0], inner_sample, inner_answer, leaf_sample)
    back = call(leaf_back, term, [leaf_half, *terms])
    near = [back] + [across(back, 2 * i, leaves) for i in range(1, lanes)]
    near = jnp.concatenate(near, axis=0)
    far = across(near, 1, leaves)

    def leaf_last(ins, outs, whole):
        near_ref, far_ref, leaf_ref, inner_ref, answer_ref, inv_ref = ins
        in_order(near_ref, far_ref, whole)
        is_leaf = height() == 0
        outs[0][...] = jnp.where(is_leaf, leaf_ref[...], inner_ref[...])
        outs[1][...] = jnp.where(is_leaf, mmt(inv_ref[...], whole[...]), answer_ref[...])

    sample, answer = call(
        leaf_last,
        [shape] * 2,
        [near, far, leaf_sample, inner_sample, inner_answer, inverse_own],
        whole_half,
    )
    return (sample[None], answer[None])


def solution(mesh):
    in_specs = (
        P("lvl", "col", None),
        P("lvl", None, "col", None),
        P("lvl", "col", None),
        P("lvl", None, None, None),
    )
    out_specs = (P("lvl", "col", None), P("lvl", "col", None))
    return jax.shard_map(
        on_device, mesh=mesh, in_specs=in_specs, out_specs=out_specs, check_vma=False
    )
```
